32 devices in a mesh: tract: 2 (over y), sky: 4 (over x, core), band: 4 (over z).
Axes of the slice: x: 2, y: 2, z: 4, core: 2. Of those that a mesh axis runs over, the one named last changes fastest.
Arguments:
- patches: float32 [8, 32, 256, 256], P(('tract', 'band'), 'sky'), parts along dimension 0, may hold values from -6 to 6
- valid_rows: int32 [8, 32], P(('tract', 'band'), 'sky'), parts along dimension 0, may hold values from 64 to 256
- slot_owner: int32 [8, 32, 1], P(('tract', 'band'), 'sky'), parts along dimension 0, may hold values from 0 to 3; in each aligned block of 8 rows (0 to 7, 8 to 15, ..., all dimensions but the last counted through in order) at most 4 rows name the same one
- slot_local: int32 [8, 32], P(('tract', 'band'), 'sky'), parts along dimension 0, may hold values from 0 to 7
- slot_visit: int32 [8, 32], P(('tract', 'band'), 'sky'), parts along dimension 0, may hold values from 0 to 11
- basis_coef: float32 [8, 12, 21], P(('tract', 'band')), parts along dimension 0, may hold values from -1.25 to 1.25
- inv_var: float32 [8, 12], P(('tract', 'band')), parts along dimension 0, may hold values from 0.1 to 1
- kernel_x: bfloat16 [21, 41], replicated, may hold values from -1 to 1
- kernel_y: bfloat16 [21, 41], replicated, may hold values from -1 to 1
Outputs:
- band_coadd: float32 [8, 32, 256, 256], P(('tract', 'band'), 'sky'), parts along dimension 0
- detection: float32 [64, 256, 256], P(('tract', 'sky'), 'band'), parts along dimension 0
The draws below stay inside these ranges and needn't reach their ends.
There are 2 independent parts, one for each index of `tract`. The reference program is written for one: setup_inputs(seed, part) draws one part's arguments, and reference() takes and returns one part's arrays. A program takes and returns all parts, laid end to end along the dimension named above; an argument that names none is the same for every part. Nothing has to cross between parts.
Inputs may be any that keep to these rules, and one draw needn't show every extreme that they name: `slot_owner`: among the pieces of one device no owner appears more than 4 times; some device gives exactly 4 pieces to one owner.
All inputs are finite; a program needn't handle non-finite values.
Results may differ from the reference program's by a relative error of at most 0.015.
Values may be sent and summed in bfloat16 or wider, within the bound.
No kernel may reach another device: no remote copies, remote signals or barrier semaphores. Data moves between devices by JAX's collectives and lax.ppermute only.
A program may use at most 128 MiB of HBM per device.

```python
import math
import jax
import jax.numpy as jnp
import numpy as np
from jax import lax

P_SIZE = 256
KS = 41
NB = 21
VIS = 12
SLOTS_DEV = 8
PATCH_DEV = 8
CAP = 4
SLOTS = 32
PATCHES = 32
BANDS = 4
N_SKY = 4


def with_ends(values, rng, smallest, largest):
    place = [jax.random.randint(jax.random.fold_in(rng, axis), (), 0, length) for axis, length in enumerate(values.shape)]
    main_axis = values.shape.index(max(values.shape))
    next_to = place[:main_axis] + [(place[main_axis] + 1) % values.shape[main_axis]] + place[main_axis + 1:]
    return values.at[tuple(place)].set(smallest).at[tuple(next_to)].set(largest)


def block_scale(stream_key, extent, shards, least, high):
    factor_of = 1.0
    for axis_at, blocks in shards:
        heights = jax.random.uniform(jax.random.fold_in(jax.random.fold_in(stream_key, 6), axis_at), (blocks,), jnp.float32, least / len(shards), high / len(shards))
        factor_of = factor_of * jnp.repeat(jnp.exp(heights), extent[axis_at] // blocks).reshape((-1,) + (1,) * (len(extent) - 1 - axis_at))
    return factor_of


def shared_out(stream_key, own, number, rows, count, top, limit, lean):
    order = jax.random.permutation(stream_key, count)
    heavy_load, common = load_shares(count, rows * top, limit, lean, True), load_shares(count, rows * top, limit, lean, False)
    places = jnp.arange(count)

    def named(sizes, offset_by):
        used = int((sizes > 0).sum())
        fixed = max(1, used // 4)
        passed = fixed + (places - fixed + offset_by * (used - fixed)) % max(1, count - fixed)
        return jnp.zeros((count,), jnp.int32).at[order[jnp.where(places < fixed, places, passed)]].set(jnp.asarray(sizes, jnp.int32))

    sizes = jnp.where(number % 4 == 0, named(heavy_load, number // 4), named(common, number - number // 4 - 1))
    mixed = jax.random.permutation(jax.random.fold_in(own, 3), count)
    donor, receiver = mixed[0:count // 2 * 2:2], mixed[1:count // 2 * 2:2]
    room = jnp.minimum(sizes[donor] - 1, limit - sizes[receiver]) // 2
    room = jnp.where((donor == order[0]) | (receiver == order[0]) | (sizes[receiver] == 0), 0, jnp.maximum(room, 0))
    passed = jax.random.randint(jax.random.fold_in(own, 4), (count // 2,), 0, 1 << 20) % (room + 1)
    sizes = sizes.at[donor].add(-passed).at[receiver].add(passed)
    items = jnp.searchsorted(jnp.cumsum(sizes), jnp.arange(rows * top), side="right").astype(jnp.int32)
    table = items.reshape(top, rows).T
    table = table[jax.random.permutation(jax.random.fold_in(own, 1), rows)]
    offset_by = jax.random.randint(jax.random.fold_in(own, 2), (rows, 1), 0, top)
    return jnp.take_along_axis(table, (jnp.arange(top)[None, :] + offset_by) % top, axis=1)


def load_shares(amount, total, reach, lean, full):
    portions = [(1 << 20) // math.isqrt(grade ** lean) + 1 for grade in range(1, amount + 1)]
    largest = reach if full else min(reach, max(-(-total // amount), total * portions[0] // sum(portions)))
    least = 1 if total - largest >= amount - 1 else 0
    given, rest = [largest] + [least] * (amount - 1), total - largest - least * (amount - 1)
    while rest > 0:
        movable = [i for i in range(1, amount) if given[i] < largest] or [i for i in range(1, amount) if given[i] < reach]
        whole, budget = sum([portions[i] for i in movable]), rest
        for i in movable:
            addition = min(reach - given[i], max(1, budget * portions[i] // whole), rest)
            given[i] = given[i] + addition
            rest = rest - addition
    return np.array(given)


def normal_values(own_key, dims, scale, limit, shards=(), held_as=jnp.bfloat16):
    gain = block_scale(own_key, dims, shards, -0.22, 0.18) if shards else 1.0
    drawn = jax.random.normal(own_key, dims, jnp.float32) * scale * gain
    return jnp.minimum(jnp.maximum(drawn, -limit), limit).astype(held_as)


def setup_inputs(seed: int = 0, part: int = 0) -> dict:
    seeds = jax.random.split(jax.random.key(seed), 10)
    own_keys = jax.random.split(jax.random.fold_in(seeds[9], part), 10)
    patches = normal_values(own_keys[0], (BANDS, SLOTS, P_SIZE, P_SIZE), 1.0, 6.0, ((0, 4), (1, 4)), jnp.float32)
    valid_rows = with_ends(jax.random.randint(own_keys[1], (BANDS, SLOTS), P_SIZE // 4, P_SIZE + 1), jax.random.fold_in(own_keys[1], 1), P_SIZE // 4, P_SIZE).astype(jnp.int32)
    slot_owner_keys = jax.random.split(jax.random.fold_in(own_keys[2], 1), BANDS * SLOTS // SLOTS_DEV)
    slot_owner_turns = jax.random.permutation(jax.random.fold_in(own_keys[2], 3), BANDS * SLOTS // SLOTS_DEV)
    slot_owner = jax.vmap(lambda own, number: shared_out(jax.random.fold_in(own_keys[2], 2), own, number, SLOTS_DEV, N_SKY, 1, CAP, 2))(slot_owner_keys, slot_owner_turns).reshape((BANDS, SLOTS, 1))
    slot_local = with_ends(jax.random.randint(own_keys[3], (BANDS, SLOTS), 0, PATCH_DEV), jax.random.fold_in(own_keys[3], 1), 0, PATCH_DEV - 1).astype(jnp.int32)
    slot_visit = with_ends(jax.random.randint(own_keys[4], (BANDS, SLOTS), 0, VIS), jax.random.fold_in(own_keys[4], 1), 0, VIS - 1).astype(jnp.int32)
    basis_coef = normal_values(own_keys[5], (BANDS, VIS, NB), NB ** -0.5, 1.25, ((0, 4),), jnp.float32)
    inv_var = jnp.clip(jnp.exp(math.log(1.0) - 2.3025851 * jax.random.uniform(own_keys[6], (BANDS, VIS), jnp.float32) ** block_scale(own_keys[6], (BANDS, VIS), ((0, 4),), -0.2, 0.2)), 0.1, 1.0)
    kernel_x = normal_values(seeds[7], (NB, KS), KS ** -0.5, 1.0)
    kernel_y = normal_values(seeds[8], (NB, KS), KS ** -0.5, 1.0)
    return dict(patches=patches, valid_rows=valid_rows, slot_owner=slot_owner, slot_local=slot_local, slot_visit=slot_visit, basis_coef=basis_coef, inv_var=inv_var, kernel_x=kernel_x, kernel_y=kernel_y)


def tables(kernel_x, kernel_y, tile_side):
    kernel_len = kernel_x.shape[1]
    half_len = kernel_len // 2
    row_ids = lax.broadcasted_iota(jnp.int32, (tile_side, tile_side, kernel_len), 0)
    col_ids = lax.broadcasted_iota(jnp.int32, (tile_side, tile_side, kernel_len), 1)
    tap_ids = lax.broadcasted_iota(jnp.int32, (tile_side, tile_side, kernel_len), 2)
    picked = (col_ids - row_ids + half_len == tap_ids).astype(jnp.float32)
    across = jnp.einsum('jma,ka->kjm', picked, kernel_x.astype(jnp.float32), precision=lax.Precision.HIGHEST).astype(jnp.bfloat16)
    down_tables = jnp.einsum('ima,ka->kim', picked, kernel_y.astype(jnp.float32), precision=lax.Precision.HIGHEST).astype(jnp.bfloat16)
    return across, down_tables


def reference(patches, valid_rows, slot_owner, slot_local, slot_visit, basis_coef, inv_var, kernel_x, kernel_y):
    across, down_tables = tables(kernel_x, kernel_y, P_SIZE)
    target = (slot_owner[:, :, 0] * PATCH_DEV + slot_local).astype(jnp.int32)
    row_ids = jnp.arange(P_SIZE, dtype=jnp.int32)

    def one_band(operands):
        band_tiles, row_count, band_target, visits, coef_band, var_band = operands
        kept_rows = row_ids[None, :] < row_count[:, None]
        masked = jnp.where(kept_rows[:, :, None], band_tiles, 0.0).astype(jnp.bfloat16)
        weight = lax.optimization_barrier(var_band[visits].astype(jnp.bfloat16)).astype(jnp.float32)
        coeffs = lax.optimization_barrier(coef_band[visits].astype(jnp.bfloat16)).astype(jnp.float32)
        mixing = lax.optimization_barrier((weight[:, None] * coeffs).astype(jnp.bfloat16)).astype(jnp.float32)
        tiles_wide = masked.astype(jnp.float32)

        def one_basis(basis):
            weighted = mixing[:, basis][:, None, None] * tiles_wide
            return jax.ops.segment_sum(weighted, band_target, num_segments=PATCHES)

        combined = lax.map(one_basis, jnp.arange(NB))
        combined = jnp.transpose(combined, (1, 0, 2, 3)).astype(jnp.bfloat16)
        section_one = jnp.einsum('pkim,kjm->pkij', combined.astype(jnp.float32), across.astype(jnp.float32)).astype(jnp.bfloat16)
        numerator = jnp.einsum('kim,pkmj->pij', down_tables.astype(jnp.float32), section_one.astype(jnp.float32))
        coverage = jax.ops.segment_sum(weight[:, None] * kept_rows.astype(jnp.float32), band_target, num_segments=PATCHES)
        return numerator / jnp.maximum(coverage, 1.0)[:, :, None]

    band_coadd = lax.map(one_band, (patches, valid_rows, target, slot_visit, basis_coef, inv_var))
    detection = jnp.sum(band_coadd, axis=0)
    return band_coadd, detection
```

```python
import functools

import jax
import jax.numpy as jnp
import ml_dtypes
import numpy as np
from jax import lax
from jax.experimental import pallas as pl
from jax.experimental.pallas import tpu as pltpu
from jax.sharding import PartitionSpec as P

PATCH_DEV = 8
F32, BF16 = jnp.float32, jnp.bfloat16
VMEM_BYTES = 52 * 1024 * 1024


def round_up(value, multiple):
    return -(-value // multiple) * multiple


def wave_tables(side, kernel_len):
    half_len = kernel_len // 2
    count = -(-(side + half_len) // 2)
    omega = np.pi * (np.arange(count) + 0.5) / count
    sub, lane = round_up(count, 16), round_up(count, 128)

    def waves(points, width):
        out = np.zeros((len(points), 2 * width), np.float64)
        out[:, :count] = np.cos(np.outer(points, omega))
        out[:, width : width + count] = np.sin(np.outer(points, omega))
        return out

    pixels, taps = np.arange(side), np.arange(kernel_len) - half_len
    held = lambda a: np.ascontiguousarray(a).astype(ml_dtypes.bfloat16)
    return dict(
        sub=sub,
        lane=lane,
        scale=1.0 / (count * count),
        to_col=held(waves(pixels, lane)),
        to_row=held(waves(pixels, sub).T),
        from_col=held(waves(pixels, lane).T),
        from_row=held(waves(pixels, sub)),
        tap_col=held(waves(taps, lane)),
        tap_row=held(waves(taps, sub).T),
    )


def dot(a, b, contract=((1,), (0,))):
    return lax.dot_general(a, b, (contract, ((), ())), preferred_element_type=F32)


def convolve_kernel(plan, owner, valid, visit, patch, coef, inv_var, kx, ky, to_col, to_row, from_col, from_row,
                    tap_col, tap_row, *rest):
    outs, (row_waves, col_waves, back) = rest[:-3], rest[-3:]
    sub, lane, rows, nb = plan["sub"], plan["lane"], plan["rows"], plan["nb"]
    slot = pl.program_id(0)
    side = patch.shape[1]

    @pl.when(slot == 0)
    def _():
        row_waves[...] = dot(tap_row[...], ky[...], ((1,), (1,)))
        col_waves[...] = (dot(kx[...], tap_col[...]) * plan["scale"]).astype(BF16)
        band = lax.axis_index("band")
        for phase, shift in enumerate(plan["shifts"]):
            start = pl.multiple_of(lax.rem(band + shift, nb) * rows, rows)
            back[phase * rows : (phase + 1) * rows, :] = from_row[pl.ds(start, rows), :]

    basis = kx.shape[0]
    weight = jnp.full((1, basis), inv_var[0, visit[slot]], F32).astype(BF16).astype(F32)
    coeff = coef[pl.ds(visit[slot], 1), :].astype(BF16).astype(F32)
    mixing = (weight * coeff).astype(BF16).astype(F32)
    row_ids = lax.broadcasted_iota(jnp.int32, (side, side), 0)
    masked = jnp.where(row_ids < valid[slot], patch[0], 0.0).astype(BF16)
    col = dot(masked, to_col[...]).astype(BF16)
    mixed = (row_waves[...] * mixing).astype(BF16)
    parts = []
    for half in range(2):
        cols = slice(0, 2 * lane)
        parts.append(dot(to_row[half * sub : (half + 1) * sub, :], col))
    resp_c = dot(mixed[:sub], col_waves[...])
    resp_s = dot(mixed[sub:], col_waves[...])
    pa, pb, qa, qb = resp_c[:, :lane], resp_c[:, lane:], resp_s[:, :lane], resp_s[:, lane:]
    cc, cs, sc, ss = parts[0][:, :lane], parts[0][:, lane:], parts[1][:, :lane], parts[1][:, lane:]
    y_cc = (pa * cc + pb * cs + qa * sc + qb * ss).astype(BF16)
    y_cs = (pa * cs - pb * cc + qa * ss - qb * sc).astype(BF16)
    y_sc = (pa * sc + pb * ss - qa * cc - qb * cs).astype(BF16)
    y_ss = (pa * ss - pb * sc - qa * cs + qb * cc).astype(BF16)
    z_c = dot(y_cc, from_col[:lane, :]) + dot(y_cs, from_col[lane:, :])
    z_s = dot(y_sc, from_col[:lane, :]) + dot(y_ss, from_col[lane:, :])
    full = (
        dot(back[:, :sub], z_c.astype(BF16)) + dot(back[:, sub:], z_s.astype(BF16))
    ).astype(BF16)

    mine = owner[slot]
    rank = jnp.int32(0)
    for other in range(plan["slots"]):
        rank = rank + jnp.where((other < slot) & (owner[other] == mine), 1, 0).astype(jnp.int32)
    me = lax.axis_index("sky")
    if plan["single"]:
        targets = [(0, mine * plan["cap"] + rank, None)]
    else:
        targets = [(g, rank, (mine ^ me) == g) for g in range(plan["sky"])]
    for group, position, taken in targets:
        first = sum(plan["outs_of"][:group])

        def store(group=group, position=position, first=first):
            if plan["outs_of"][group] == 1:
                for phase in range(nb):
                    outs[first][phase, position] = full[phase * rows : (phase + 1) * rows, :]
            else:
                for phase in range(nb):
                    outs[first + phase][0, position] = full[phase * rows : (phase + 1) * rows, :]

        if taken is None:
            store()
        else:
            pl.when(taken)(store)


def sum_kernel(plan, phase, *refs):
    sky, nb, rows, cap, slots = plan["sky"], plan["nb"], plan["rows"], plan["cap"], plan["slots"]
    last = phase == nb - 1
    refs = list(refs)
    take = lambda n: [refs.pop(0) for _ in range(n)]
    metas = take(plan["n_meta"])
    (inv_var,) = take(1)
    boxes = take(len(plan["outs_of"]))
    arrived = take(nb - 1) if last else []
    if phase:
        take(1)
    band_out, extra, acc, cov, sem = refs
    me = lax.axis_index("sky")
    chunk = lax.rem(lax.axis_index("band") + plan["shifts"][phase], nb)
    acc[...] = jnp.zeros_like(acc)
    cov[...] = jnp.zeros_like(cov)
    row_ids = chunk * rows + lax.broadcasted_iota(jnp.int32, (rows, 128), 0)
    for source in range(sky):
        group, base = (0, source * cap) if plan["single"] else (source, 0)
        meta = lambda line, slot: (metas[0][source, line, slot] if plan["single"] else metas[source][line, slot])

        def step(slot, rank):
            here = meta(0, slot) == me

            @pl.when(here)
            def _():
                local = meta(1, slot)
                acc[local] += boxes[group][0, base + rank].astype(F32)
                weight = jnp.full((rows, 128), inv_var[0, meta(3, slot)], F32).astype(BF16).astype(F32)
                cov[local] += jnp.where(row_ids < meta(2, slot), weight, 0.0)

            return rank + jnp.where(here, 1, 0).astype(jnp.int32)

        lax.fori_loop(0, slots, step, jnp.int32(0))
    width = acc.shape[2]
    for patch in range(PATCH_DEV):
        factor = 1.0 / jnp.maximum(cov[patch], 1.0)
        for at in range(0, width, 128):
            value = acc[patch, :, at : at + 128] * factor
            acc[patch, :, at : at + 128] = value
            if last:
                for other in arrived:
                    value = value + other[patch, :, at : at + 128].astype(F32)
            extra[patch, :, at : at + 128] = value.astype(extra.dtype)
    copy = pltpu.make_async_copy(acc, band_out.at[:, pl.ds(pl.multiple_of(chunk * rows, rows), rows), :], sem)
    copy.start()
    copy.wait()


def per_device(patches, valid_rows, slot_owner, slot_local, slot_visit, basis_coef, inv_var, kernel_x, kernel_y):
    tiles = patches[0]
    slots, side, width = tiles.shape
    sky, nb = lax.axis_size("sky"), lax.axis_size("band")
    cap = max(2, 2 * slots // sky)
    rows = side // nb
    single = sky > 4 or sky & (sky - 1) != 0
    tables = wave_tables(side, kernel_x.shape[1])
    sub, lane = tables["sub"], tables["lane"]
    shifts = sorted(range(1, nb), key=lambda k: -min(k, nb - k)) + [0]
    near = 0 if single else min(2, sky)
    outs_of = [nb] if single else [1 if r < near else nb for r in range(sky)]
    box = (sky * cap if single else cap, rows, width)
    plan = dict(sub=sub, lane=lane, rows=rows, nb=nb, shifts=shifts, scale=tables["scale"], slots=slots, cap=cap,
                sky=sky, single=single, outs_of=outs_of, n_meta=1 if single else sky)
    meta = jnp.stack([slot_owner[0, :, 0], slot_local[0], valid_rows[0], slot_visit[0]])
    smem = pl.BlockSpec(memory_space=pltpu.SMEM)
    whole = lambda shape: pl.BlockSpec(shape, lambda *_: (0,) * len(shape))
    consts = [jnp.asarray(tables[n]) for n in ("to_col", "to_row", "from_col", "from_row", "tap_col", "tap_row")]
    out_shapes = []
    for n in outs_of:
        out_shapes += [jax.ShapeDtypeStruct((nb,) + box, BF16)] if n == 1 else [
            jax.ShapeDtypeStruct((1,) + box, BF16)] * nb
    coef, basis = basis_coef[0], kernel_x.shape[0]
    sent = pl.pallas_call(
        functools.partial(convolve_kernel, plan),
        grid=(slots,),
        out_shape=out_shapes,
        in_specs=[smem, smem, smem, pl.BlockSpec((1, side, width), lambda s: (s, 0, 0)), whole(coef.shape), smem,
                  whole(kernel_x.shape), whole(kernel_y.shape)] + [whole(c.shape) for c in consts],
        out_specs=[whole(o.shape) for o in out_shapes],
        scratch_shapes=[pltpu.VMEM((2 * sub, basis), F32), pltpu.VMEM((basis, 2 * lane), BF16),
                        pltpu.VMEM((side, 2 * sub), BF16)],
        compiler_params=pltpu.CompilerParams(vmem_limit_bytes=VMEM_BYTES),
        cost_estimate=pl.CostEstimate(flops=slots * 22 * side**3, bytes_accessed=slots * side * side * 6,
                                      transcendentals=0),
        name="convolve",
    )(slot_owner[0, :, 0], valid_rows[0], slot_visit[0], tiles, coef, inv_var, kernel_x, kernel_y, *consts)

    if single:
        metas = [lax.all_gather(meta, "sky")]
        boxes = [[lax.all_to_all(s, "sky", split_axis=1, concat_axis=1, tiled=True)] for s in sent]
        boxes = [[b[0], 0] for b in boxes]
        at_phase = lambda phase: [boxes[phase]]
    else:
        swap = lambda a, r: a if r == 0 else lax.ppermute(a, "sky", [(i, i ^ r) for i in range(sky)])
        metas = [swap(meta, r) for r in range(sky)]
        groups, first = [], 0
        for n in outs_of:
            groups.append(sent[first : first + n])
            first += n
        moved = [None] * sky
        for r in range(near):
            moved[r] = [swap(groups[r][0], r)]
        for r in range(near, sky):
            moved[r] = []
        for phase in range(nb):
            for r in range(near, sky):
                moved[r].append(swap(groups[r][phase], r))
        at_phase = lambda phase: [(moved[r][0], phase) if r < near else (moved[r][phase], 0) for r in range(sky)]

    band_buf, arrived, detection = None, [], None
    band_shape = jax.ShapeDtypeStruct((PATCH_DEV, side, width), F32)
    hbm = pl.BlockSpec(memory_space=pl.ANY)
    for phase in range(nb):
        last = phase == nb - 1
        pieces = at_phase(phase)
        args = metas + [inv_var] + [b for b, _ in pieces] + (arrived if last else [])
        specs = [smem] * (len(metas) + 1)
        specs += [pl.BlockSpec((1,) + box, lambda i, at=at: (at, 0, 0, 0)) for _, at in pieces]
        chunk_shape = (PATCH_DEV, rows, width)
        specs += [whole(chunk_shape)] * (len(arrived) if last else 0)
        aliases = {}
        if phase:
            aliases = {len(args): 0}
            args, specs = args + [band_buf], specs + [hbm]
        band_buf, extra = pl.pallas_call(
            functools.partial(sum_kernel, plan, phase),
            grid=(1,),
            out_shape=[band_shape, jax.ShapeDtypeStruct(chunk_shape, F32 if last else BF16)],
            in_specs=specs,
            out_specs=[hbm, whole(chunk_shape)],
            scratch_shapes=[pltpu.VMEM(chunk_shape, F32), pltpu.VMEM((PATCH_DEV, rows, 128), F32),
                            pltpu.SemaphoreType.DMA],
            input_output_aliases=aliases,
            compiler_params=pltpu.CompilerParams(vmem_limit_bytes=VMEM_BYTES),
            cost_estimate=pl.CostEstimate(flops=4 * PATCH_DEV * rows * width, bytes_accessed=12 * PATCH_DEV * rows * width,
                                          transcendentals=0),
            name="add_up",
        )(*args)
        if last:
            detection = extra
        else:
            shift = shifts[phase]
            arrived.append(lax.ppermute(extra, "band", [(b, (b + shift) % nb) for b in range(nb)]))
    return (band_buf[None], detection)


def solution(mesh):
    in_specs = (
        P(("tract", "band"), "sky", None, None),
        P(("tract", "band"), "sky"),
        P(("tract", "band"), "sky", None),
        P(("tract", "band"), "sky"),
        P(("tract", "band"), "sky"),
        P(("tract", "band"), None, None),
        P(("tract", "band"), None),
        P(),
        P(),
    )
    out_specs = (P(("tract", "band"), "sky", None, None), P(("tract", "sky"), "band", None))
    return jax.shard_map(per_device, mesh=mesh, in_specs=in_specs, out_specs=out_specs, check_vma=False)
```

```python
import functools

import jax
import jax.numpy as jnp
import ml_dtypes
import numpy as np
from jax import lax
from jax.experimental import pallas as pl
from jax.experimental.pallas import tpu as pltpu
from jax.sharding import PartitionSpec as P

PATCH_DEV = 8
F32, BF16 = jnp.float32, jnp.bfloat16
MIB = 1024 * 1024
HEAD = 16
UNROLL = 2


def round_up(value, multiple):
    return -(-value // multiple) * multiple


def wave_tables(side, kernel_len):
    half_len = kernel_len // 2
    count = -(-(side + half_len) // 2)
    omega = np.pi * (np.arange(count) + 0.5) / count
    sub, lane = round_up(count, 16), round_up(count, 128)

    def waves(points, width):
        out = np.zeros((len(points), 2 * width), np.float64)
        out[:, :count] = np.cos(np.outer(points, omega))
        out[:, width : width + count] = np.sin(np.outer(points, omega))
        return out

    pixels, taps = np.arange(side), np.arange(kernel_len) - half_len
    held = lambda a: np.ascontiguousarray(a).astype(ml_dtypes.bfloat16)
    return dict(
        sub=sub,
        lane=lane,
        scale=1.0 / (count * count),
        to_col=held(waves(pixels, lane)),
        to_row=held(waves(pixels, sub).T),
        from_col=held(waves(pixels, lane).T),
        from_row=held(waves(pixels, sub)),
        tap_col=held(waves(taps, lane)),
        tap_row=held(waves(taps, sub).T),
    )


def dot(a, b, contract=((1,), (0,))):
    return lax.dot_general(a, b, (contract, ((), ())), preferred_element_type=F32)


def weigh(rows, tables):
    lane = rows[0].shape[1] // 2
    (c, s), (tc, ts) = rows, tables
    cc, cs, sc, ss = c[:, :lane], c[:, lane:], s[:, :lane], s[:, lane:]
    pa, pb, qa, qb = tc[:, :lane], tc[:, lane:], ts[:, :lane], ts[:, lane:]
    return (
        (pa * cc + pb * cs + qa * sc + qb * ss).astype(BF16),
        (pa * cs - pb * cc + qa * ss - qb * sc).astype(BF16),
        (pa * sc + pb * ss - qa * cc - qb * cs).astype(BF16),
        (pa * ss - pb * sc - qa * cs + qb * cc).astype(BF16),
    )


def convolve_kernel(plan, *refs):
    n_in, n_out = plan["n_in"], plan["n_out"]
    sources, outs, held = refs[:n_in], refs[n_in : n_in + n_out], refs[n_in + n_out :]
    local, (sems, row_waves, col_waves, back, heads) = held[:n_in], held[n_in:]
    sub, lane, rows, nb, cap, slots = (plan[k] for k in ("sub", "lane", "rows", "nb", "cap", "slots"))
    copies = [pltpu.make_async_copy(a, b, sems.at[i]) for i, (a, b) in enumerate(zip(sources[:-1], local[:-1]))]
    tiles = [
        pltpu.make_async_copy(sources[-1].at[s], local[-1].at[s], sems.at[n_in - 1 + s]) for s in range(slots)
    ]
    for copy in copies + tiles:
        copy.start()
    owner, local_id, valid, visit, inv_var, coef, kx, ky, to_col, to_row, from_col, from_row, tap_col, tap_row, patch = local
    for copy in copies:
        copy.wait()
    side = patch.shape[1]
    row_waves[...] = dot(tap_row[...], ky[...], ((1,), (1,)))
    col_waves[...] = (dot(kx[...], tap_col[...]) * plan["scale"]).astype(BF16)
    band = lax.axis_index("band")
    for phase in range(nb):
        start = pl.multiple_of(plan["chunk"](band, phase) * rows, rows)
        back[phase * rows : (phase + 1) * rows, :] = from_row[pl.ds(start, rows), :]
    heads[...] = jnp.full(heads.shape, -1.0, F32)
    me = lax.axis_index("sky")
    basis = kx.shape[0]
    lanes = lax.broadcasted_iota(jnp.int32, (1, 128), 1)

    def convolved(slot):
        seen = visit[0, slot]
        weight = jnp.full((1, basis), inv_var[0, seen], F32).astype(BF16).astype(F32)
        mixing = (weight * coef[seen].astype(BF16).astype(F32)).astype(BF16).astype(F32)
        row_ids = lax.broadcasted_iota(jnp.int32, (side, side), 0)
        masked = jnp.where(row_ids < valid[0, slot], patch[slot], 0.0).astype(BF16)
        col = dot(masked, to_col[...]).astype(BF16)
        mixed = (row_waves[...] * mixing).astype(BF16)
        parts = (dot(to_row[:sub, :], col), dot(to_row[sub:, :], col))
        tables = (dot(mixed[:sub], col_waves[...]), dot(mixed[sub:], col_waves[...]))
        y_cc, y_cs, y_sc, y_ss = weigh(parts, tables)
        z_c = dot(y_cc, from_col[:lane, :]) + dot(y_cs, from_col[lane:, :])
        z_s = dot(y_sc, from_col[:lane, :]) + dot(y_ss, from_col[lane:, :])
        return (dot(back[:, :sub], z_c.astype(BF16)) + dot(back[:, sub:], z_s.astype(BF16))).astype(BF16)

    def deliver(slot, full):
        mine = owner[0, slot]
        rank = jnp.int32(0)
        for other in range(slots):
            rank = rank + jnp.where((other < slot) & (owner[0, other] == mine), 1, 0).astype(jnp.int32)
        box = mine if plan["single"] else mine ^ me
        weight = jnp.full((1, 128), inv_var[0, visit[0, slot]], F32)
        facts = jnp.where(lanes == 8 * rank, local_id[0, slot].astype(F32), heads[box])
        facts = jnp.where(lanes == 8 * rank + 1, valid[0, slot].astype(F32), facts)
        heads[box] = jnp.where(lanes == 8 * rank + 2, weight, facts)
        for group in range(len(plan["split"])):
            at = mine if plan["single"] else 0

            def store(group=group, at=at):
                for phase in range(nb):
                    ref, first = plan["place"](outs, group, phase)
                    start = pl.multiple_of(first + rank * rows, rows)
                    ref[at, pl.ds(start, rows), :] = full[phase * rows : (phase + 1) * rows, :]

            if plan["single"]:
                store()
            else:
                pl.when(box == group)(store)

    def some(step, carry):
        slots_now = [step * UNROLL + u for u in range(UNROLL)]
        for s in slots_now:
            pltpu.make_async_copy(sources[-1].at[s], local[-1].at[s], sems.at[n_in - 1 + s]).wait()
        results = [convolved(s) for s in slots_now]
        for s, full in zip(slots_now, results):
            deliver(s, full)
        return carry

    lax.fori_loop(0, slots // UNROLL, some, 0)
    width = patch.shape[2]
    for group in range(len(plan["split"])):
        ref, first = plan["head"](outs, group)
        for at in range(ref.shape[0]):
            row = heads[at if plan["single"] else group]
            row = jnp.concatenate([row] * (width // 128), axis=1)
            ref[at, first : first + HEAD, :] = jnp.broadcast_to(row, (HEAD, width)).astype(BF16)


def sum_kernel(plan, phase, *refs):
    sky, nb, rows, cap, per = plan["sky"], plan["nb"], plan["rows"], plan["cap"], plan["per"]
    first, last = phase == 0, phase == nb - 1
    refs = list(refs)
    take = lambda n: [refs.pop(0) for _ in range(n)]
    boxes = take(len(plan["split"]))
    arrived = take(len(plan["adds"][phase]))
    heads = take(len(plan["split"])) if first else None
    facts = None if first else take(2)
    if not first:
        take(1)
    band_out, extra = take(2)
    if first:
        facts = take(2)
    acc, cov, sems = take(3)
    if first:
        whole_facts, weights = take(2)
        rows_of = [h[d, 0:1, :128].astype(F32) for h in heads for d in range(h.shape[0])]
        for source, row in enumerate(rows_of):
            whole_facts[source : source + 1, :] = row.astype(jnp.int32)
            weights[source : source + 1, :] = row
        copies = [pltpu.make_async_copy(a, b, sems.at[i]) for i, (a, b) in enumerate(((whole_facts, facts[0]), (weights, facts[1])))]
        for copy in copies:
            copy.start()
    chunk = plan["chunk"](lax.axis_index("band"), phase)
    acc[...] = jnp.zeros_like(acc)
    cov[...] = jnp.zeros_like(cov)
    row_ids = chunk * rows + lax.broadcasted_iota(jnp.int32, (rows, 128), 0)
    if first:
        for copy in copies:
            copy.wait()
    for source in range(sky):
        group, at = (0, source) if plan["single"] else (source, 0)
        for rank in range(cap):
            local = facts[0][source, 8 * rank]

            @pl.when(local >= 0)
            def _(group=group, at=at, rank=rank, source=source, local=local):
                acc[local] += boxes[group][at, rank * rows : (rank + 1) * rows, :].astype(F32)
                weight = jnp.full((rows, 128), facts[1][source, 8 * rank + 2], F32)
                cov[local] += jnp.where(row_ids < facts[0][source, 8 * rank + 1], weight, 0.0)

    width = acc.shape[2]
    copies = []
    for patch in range(per):
        factor = 1.0 / jnp.maximum(cov[patch], 1.0)
        for at in range(0, width, 128):
            value = acc[patch, :, at : at + 128] * factor
            acc[patch, :, at : at + 128] = value
            for other in arrived:
                value = value + other[patch, :, at : at + 128].astype(F32)
            extra[patch, :, at : at + 128] = value.astype(extra.dtype)
        copies.append(pltpu.make_async_copy(
            acc.at[patch], band_out.at[patch, pl.ds(pl.multiple_of(chunk * rows, rows), rows), :], sems.at[patch]))
        copies[-1].start()
    for copy in copies:
        copy.wait()


def band_plan(nb):
    if nb == 4:
        masks = [3, 2, 1, 0]
        chunk = lambda band, phase: band ^ masks[phase]
        partner = lambda band, phase: band ^ (1, 2, 1)[phase]
        adds = [[], [0], [], [1, 2]]
    else:
        shifts = sorted(range(1, nb), key=lambda k: -min(k, nb - k)) + [0]
        chunk = lambda band, phase: (band + shifts[phase]) % nb if isinstance(band, int) else lax.rem(band + shifts[phase], nb)
        partner = chunk
        adds = [[]] * (nb - 1) + [list(range(nb - 1))]
    return chunk, partner, adds


def per_device(patches, valid_rows, slot_owner, slot_local, slot_visit, basis_coef, inv_var, kernel_x, kernel_y):
    tiles = patches[0]
    slots, side, width = tiles.shape
    sky, nb = lax.axis_size("sky"), lax.axis_size("band")
    cap = max(2, 2 * slots // sky)
    rows = side // nb
    single = sky > 4 or sky & (sky - 1) != 0
    tables = wave_tables(side, kernel_x.shape[1])
    sub, lane = tables["sub"], tables["lane"]
    chunk, partner, adds = band_plan(nb)
    near = 0 if single else min(2, sky)
    split = [True] if single else [r >= near for r in range(sky)]
    n_dest = sky if single else 1
    box = cap * rows
    out_shapes, first_out = [], []
    for cut in split:
        first_out.append(len(out_shapes))
        heights = [box + (HEAD if phase == 0 else 0) for phase in range(nb)] if cut else [nb * box + HEAD]
        out_shapes += [jax.ShapeDtypeStruct((n_dest, h, width), BF16) for h in heights]

    def place(outs, group, phase):
        return (outs[first_out[group] + phase], 0) if split[group] else (outs[first_out[group]], phase * box)

    def head(outs, group):
        return outs[first_out[group]], box if split[group] else nb * box

    plan = dict(sub=sub, lane=lane, rows=rows, nb=nb, scale=tables["scale"], slots=slots, cap=cap, sky=sky, per=PATCH_DEV,
                single=single, split=split, place=place, head=head, chunk=chunk, adds=adds)
    smem = pl.BlockSpec(memory_space=pltpu.SMEM)
    hbm = pl.BlockSpec(memory_space=pltpu.HBM)
    vmem = pl.BlockSpec(memory_space=pltpu.VMEM)
    consts = [jnp.asarray(tables[n]) for n in ("to_col", "to_row", "from_col", "from_row", "tap_col", "tap_row")]
    weights = lax.reduce_precision(inv_var, 8, 7)
    args = [slot_owner.reshape(1, slots), slot_local, valid_rows, slot_visit, weights, basis_coef.transpose(1, 0, 2),
            kernel_x, kernel_y] + consts + [tiles]
    plan.update(n_in=len(args), n_out=len(out_shapes))
    landing = [pltpu.SMEM(a.shape, a.dtype) for a in args[:5]] + [pltpu.VMEM(a.shape, a.dtype) for a in args[5:]]
    sent = pl.pallas_call(
        functools.partial(convolve_kernel, plan),
        out_shape=out_shapes,
        in_specs=[hbm] * len(args),
        out_specs=[vmem] * len(out_shapes),
        scratch_shapes=landing + [
            pltpu.SemaphoreType.DMA((len(args) - 1 + slots,)), pltpu.VMEM((2 * sub, kernel_x.shape[0]), F32),
            pltpu.VMEM((kernel_x.shape[0], 2 * lane), BF16), pltpu.VMEM((side, 2 * sub), BF16),
            pltpu.VMEM((sky, 1, 128), F32)],
        compiler_params=pltpu.CompilerParams(vmem_limit_bytes=40 * MIB),
        cost_estimate=pl.CostEstimate(flops=slots * 22 * side**3, bytes_accessed=slots * side * side * 6,
                                      transcendentals=0),
        name="convolve",
    )(*args)

    swap = lambda a, r: a if r == 0 else lax.ppermute(a, "sky", [(i, i ^ r) for i in range(sky)])
    moved = list(sent)
    if single:
        moved = [lax.all_to_all(s, "sky", split_axis=0, concat_axis=0, tiled=True) for s in sent]
    else:
        for r in range(1, near):
            moved[first_out[r]] = swap(sent[first_out[r]], r)
        for phase in range(nb):
            for r in range(near, sky):
                moved[first_out[r] + phase] = swap(sent[first_out[r] + phase], r)

    band_buf, facts, arrived = None, None, []
    band_shape = jax.ShapeDtypeStruct((PATCH_DEV, side, width), F32)
    chunk_shape = (PATCH_DEV, rows, width)
    whole = lambda shape: pl.BlockSpec(shape, lambda *_: (0,) * len(shape))
    fact_shapes = [jax.ShapeDtypeStruct((sky, 128), jnp.int32), jax.ShapeDtypeStruct((sky, 128), F32)]
    for phase in range(nb):
        first, last = phase == 0, phase == nb - 1
        inputs, specs = [], []
        for group, cut in enumerate(split):
            inputs.append(place(moved, group, phase)[0])
            specs.append(pl.BlockSpec((n_dest, box, width), lambda i, at=0 if cut else phase: (0, at, 0)))
        for earlier in adds[phase]:
            inputs.append(arrived[earlier])
            specs.append(whole(chunk_shape))
        outs = [band_shape, jax.ShapeDtypeStruct(chunk_shape, F32 if last else BF16)]
        out_specs, aliases, scratch = [hbm, whole(chunk_shape)], {}, []
        if first:
            for group in range(len(split)):
                ref, start = head(moved, group)
                inputs.append(ref)
                specs.append(pl.BlockSpec((n_dest, HEAD, width), lambda i, at=start // HEAD: (0, at, 0)))
            outs, out_specs = outs + fact_shapes, out_specs + [smem] * 2
            scratch = [pltpu.VMEM(s.shape, s.dtype) for s in fact_shapes]
        else:
            inputs, specs = inputs + facts, specs + [smem] * 2
            aliases = {len(inputs): 0}
            inputs, specs = inputs + [band_buf], specs + [hbm]
        band_buf, extra, *rest = pl.pallas_call(
            functools.partial(sum_kernel, plan, phase),
            grid=(1,),
            out_shape=outs,
            in_specs=specs,
            out_specs=out_specs,
            scratch_shapes=[pltpu.VMEM(chunk_shape, F32), pltpu.VMEM((PATCH_DEV, rows, 128), F32),
                            pltpu.SemaphoreType.DMA((PATCH_DEV,))] + scratch,
            input_output_aliases=aliases,
            compiler_params=pltpu.CompilerParams(vmem_limit_bytes=24 * MIB),
            cost_estimate=pl.CostEstimate(flops=4 * PATCH_DEV * rows * width,
                                          bytes_accessed=12 * PATCH_DEV * rows * width, transcendentals=0),
            name="add_up",
        )(*inputs)
        facts = rest if first else facts
        if not last:
            arrived.append(lax.ppermute(extra, "band", [(b, partner(b, phase)) for b in range(nb)]))
    return (band_buf[None], extra)


def solution(mesh):
    in_specs = (
        P(("tract", "band"), "sky", None, None),
        P(("tract", "band"), "sky"),
        P(("tract", "band"), "sky", None),
        P(("tract", "band"), "sky"),
        P(("tract", "band"), "sky"),
        P(("tract", "band"), None, None),
        P(("tract", "band"), None),
        P(),
        P(),
    )
    out_specs = (P(("tract", "band"), "sky", None, None), P(("tract", "sky"), "band", None))
    return jax.shard_map(per_device, mesh=mesh, in_specs=in_specs, out_specs=out_specs, check_vma=False)
```

```python
import functools

import jax
import jax.numpy as jnp
import ml_dtypes
import numpy as np
from jax import lax
from jax.experimental import pallas as pl
from jax.experimental.pallas import tpu as pltpu
from jax.sharding import PartitionSpec as P

PATCH_DEV = 8
F32, BF16 = jnp.float32, jnp.bfloat16
MIB = 1024 * 1024
HEAD = 16
UNROLL = 4
CONV_VMEM = 64
SUM_VMEM = 24


def round_up(value, multiple):
    return -(-value // multiple) * multiple


def wave_tables(side, kernel_len):
    half_len = kernel_len // 2
    count = -(-(side + half_len) // 2)
    omega = np.pi * (np.arange(count) + 0.5) / count
    sub, lane = round_up(count, 16), round_up(count, 128)

    def waves(points, width):
        out = np.zeros((len(points), 2 * width), np.float64)
        out[:, :count] = np.cos(np.outer(points, omega))
        out[:, width : width + count] = np.sin(np.outer(points, omega))
        return out

    pixels, taps = np.arange(side), np.arange(kernel_len) - half_len
    held = lambda a: np.ascontiguousarray(a).astype(ml_dtypes.bfloat16)
    return dict(
        sub=sub,
        lane=lane,
        scale=1.0 / (count * count),
        to_col=held(waves(pixels, lane)),
        to_row=held(waves(pixels, sub).T),
        from_col=held(waves(pixels, lane).T),
        from_row=held(waves(pixels, sub)),
        tap_col=held(waves(taps, lane)),
        tap_row=held(waves(taps, sub).T),
    )


def dot(a, b, contract=((1,), (0,))):
    return lax.dot_general(a, b, (contract, ((), ())), preferred_element_type=F32)


def weigh(rows, tables):
    lane = rows[0].shape[1] // 2
    (c, s), (tc, ts) = rows, tables
    cc, cs, sc, ss = c[:, :lane], c[:, lane:], s[:, :lane], s[:, lane:]
    pa, pb, qa, qb = tc[:, :lane], tc[:, lane:], ts[:, :lane], ts[:, lane:]
    return (
        (pa * cc + pb * cs + qa * sc + qb * ss).astype(BF16),
        (pa * cs - pb * cc + qa * ss - qb * sc).astype(BF16),
        (pa * sc + pb * ss - qa * cc - qb * cs).astype(BF16),
        (pa * ss - pb * sc - qa * cs + qb * cc).astype(BF16),
    )


def convolve_kernel(plan, *refs):
    n_in, n_out = plan["n_in"], plan["n_out"]
    sources, outs, held = refs[:n_in], refs[n_in : n_in + n_out], refs[n_in + n_out :]
    local, (sems, out_sems, row_waves, col_waves, back, heads, done, head_rows) = held[:n_in], held[n_in:]
    sub, lane, rows, nb, cap, slots = (plan[k] for k in ("sub", "lane", "rows", "nb", "cap", "slots"))
    copies = [pltpu.make_async_copy(a, b, sems.at[i]) for i, (a, b) in enumerate(zip(sources[:-1], local[:-1]))]
    tiles = [
        pltpu.make_async_copy(sources[-1].at[s], local[-1].at[s], sems.at[n_in - 1 + s]) for s in range(slots)
    ]
    for copy in copies + tiles:
        copy.start()
    owner, local_id, valid, visit, inv_var, coef, kx, ky, to_col, to_row, from_col, from_row, tap_col, tap_row, patch = local
    for copy in copies:
        copy.wait()
    side = patch.shape[1]
    row_waves[...] = dot(tap_row[...], ky[...], ((1,), (1,)))
    col_waves[...] = (dot(kx[...], tap_col[...]) * plan["scale"]).astype(BF16)
    band = lax.axis_index("band")
    for phase in range(nb):
        start = pl.multiple_of(plan["chunk"](band, phase) * rows, rows)
        back[phase * rows : (phase + 1) * rows, :] = from_row[pl.ds(start, rows), :]
    heads[...] = jnp.full(heads.shape, -1.0, F32)
    me = lax.axis_index("sky")
    basis = kx.shape[0]
    lanes = lax.broadcasted_iota(jnp.int32, (1, 128), 1)

    def convolved(slot):
        seen = visit[0, slot]
        weight = jnp.full((1, basis), inv_var[0, seen], F32).astype(BF16).astype(F32)
        mixing = (weight * coef[seen].astype(BF16).astype(F32)).astype(BF16).astype(F32)
        row_ids = lax.broadcasted_iota(jnp.int32, (side, side), 0)
        masked = jnp.where(row_ids < valid[0, slot], patch[slot], 0.0).astype(BF16)
        col = dot(masked, to_col[...]).astype(BF16)
        mixed = (row_waves[...] * mixing).astype(BF16)
        parts = (dot(to_row[:sub, :], col), dot(to_row[sub:, :], col))
        tables = (dot(mixed[:sub], col_waves[...]), dot(mixed[sub:], col_waves[...]))
        y_cc, y_cs, y_sc, y_ss = weigh(parts, tables)
        z_c = dot(y_cc, from_col[:lane, :]) + dot(y_cs, from_col[lane:, :])
        z_s = dot(y_sc, from_col[:lane, :]) + dot(y_ss, from_col[lane:, :])
        return (dot(back[:, :sub], z_c.astype(BF16)) + dot(back[:, sub:], z_s.astype(BF16))).astype(BF16)

    def sent(slot, phase, ref):
        return pltpu.make_async_copy(done.at[slot, phase * rows : (phase + 1) * rows, :], ref, out_sems.at[slot, phase])

    def deliver(slot, full):
        done[slot] = full
        mine = owner[0, slot]
        rank = jnp.int32(0)
        for other in range(slots):
            rank = rank + jnp.where((other < slot) & (owner[0, other] == mine), 1, 0).astype(jnp.int32)
        box = mine if plan["single"] else mine ^ me
        weight = jnp.full((1, 128), inv_var[0, visit[0, slot]], F32)
        facts = jnp.where(lanes == 8 * rank, local_id[0, slot].astype(F32), heads[box])
        facts = jnp.where(lanes == 8 * rank + 1, valid[0, slot].astype(F32), facts)
        heads[box] = jnp.where(lanes == 8 * rank + 2, weight, facts)
        for group in range(len(plan["split"])):
            at = mine if plan["single"] else 0

            def store(group=group, at=at):
                for phase in range(nb):
                    ref, first = plan["place"](outs, group, phase)
                    start = pl.multiple_of(first + rank * rows, rows)
                    sent(slot, phase, ref.at[at, pl.ds(start, rows), :]).start()

            if plan["single"]:
                store()
            else:
                pl.when(box == group)(store)

    def some(step, carry):
        slots_now = [step * UNROLL + u for u in range(UNROLL)]
        for s in slots_now:
            pltpu.make_async_copy(sources[-1].at[s], local[-1].at[s], sems.at[n_in - 1 + s]).wait()
        results = [convolved(s) for s in slots_now]
        for s, full in zip(slots_now, results):
            deliver(s, full)
        return carry

    lax.fori_loop(0, slots // UNROLL, some, 0)
    width = patch.shape[2]
    copies = []
    for group in range(len(plan["split"])):
        ref, first = plan["head"](outs, group)
        for at in range(ref.shape[0]):
            index = at if plan["single"] else group
            row = jnp.concatenate([heads[index]] * (width // 128), axis=1)
            head_rows[index] = jnp.broadcast_to(row, (HEAD, width)).astype(BF16)
            copies.append(pltpu.make_async_copy(
                head_rows.at[index], ref.at[at, first : first + HEAD, :], sems.at[index]))
            copies[-1].start()
    for copy in copies:
        copy.wait()
    for slot in range(slots):
        for phase in range(nb):
            sent(slot, phase, plan["place"](outs, 0, phase)[0].at[0, 0:rows, :]).wait()


def sum_kernel(plan, phase, *refs):
    sky, nb, rows, cap, per = plan["sky"], plan["nb"], plan["rows"], plan["cap"], plan["per"]
    first, last = phase == 0, phase == nb - 1
    refs = list(refs)
    take = lambda n: [refs.pop(0) for _ in range(n)]
    boxes = take(len(plan["split"]))
    arrived = take(len(plan["adds"][phase]))
    heads = take(len(plan["split"])) if first else None
    facts = None if first else take(2)
    if not first:
        take(1)
    band_out, extra = take(2)
    if first:
        facts = take(2)
    acc, cov, sems = take(3)
    if first:
        whole_facts, weights = take(2)
        rows_of = [h[d, 0:1, :128].astype(F32) for h in heads for d in range(h.shape[0])]
        for source, row in enumerate(rows_of):
            whole_facts[source : source + 1, :] = row.astype(jnp.int32)
            weights[source : source + 1, :] = row
        copies = [pltpu.make_async_copy(a, b, sems.at[i]) for i, (a, b) in enumerate(((whole_facts, facts[0]), (weights, facts[1])))]
        for copy in copies:
            copy.start()
    chunk = plan["chunk"](lax.axis_index("band"), phase)
    acc[...] = jnp.zeros_like(acc)
    cov[...] = jnp.zeros_like(cov)
    row_ids = chunk * rows + lax.broadcasted_iota(jnp.int32, (rows, 128), 0)
    if first:
        for copy in copies:
            copy.wait()
    for source in range(sky):
        group, at = (0, source) if plan["single"] else (source, 0)
        for rank in range(cap):
            local = facts[0][source, 8 * rank]

            @pl.when(local >= 0)
            def _(group=group, at=at, rank=rank, source=source, local=local):
                acc[local] += boxes[group][at, rank * rows : (rank + 1) * rows, :].astype(F32)
                weight = jnp.full((rows, 128), facts[1][source, 8 * rank + 2], F32)
                cov[local] += jnp.where(row_ids < facts[0][source, 8 * rank + 1], weight, 0.0)

    width = acc.shape[2]
    copies = []
    for patch in range(per):
        factor = 1.0 / jnp.maximum(cov[patch], 1.0)
        for at in range(0, width, 128):
            value = acc[patch, :, at : at + 128] * factor
            acc[patch, :, at : at + 128] = value
            for other in arrived:
                value = value + other[patch, :, at : at + 128].astype(F32)
            extra[patch, :, at : at + 128] = value.astype(extra.dtype)
        copies.append(pltpu.make_async_copy(
            acc.at[patch], band_out.at[patch, pl.ds(pl.multiple_of(chunk * rows, rows), rows), :], sems.at[patch]))
        copies[-1].start()
    for copy in copies:
        copy.wait()


def band_plan(nb):
    if nb == 4:
        masks = [3, 2, 1, 0]
        chunk = lambda band, phase: band ^ masks[phase]
        partner = lambda band, phase: band ^ (1, 2, 1)[phase]
        adds = [[], [0], [], [1, 2]]
    else:
        shifts = sorted(range(1, nb), key=lambda k: -min(k, nb - k)) + [0]
        chunk = lambda band, phase: (band + shifts[phase]) % nb if isinstance(band, int) else lax.rem(band + shifts[phase], nb)
        partner = chunk
        adds = [[]] * (nb - 1) + [list(range(nb - 1))]
    return chunk, partner, adds


def per_device(patches, valid_rows, slot_owner, slot_local, slot_visit, basis_coef, inv_var, kernel_x, kernel_y):
    tiles = patches[0]
    slots, side, width = tiles.shape
    sky, nb = lax.axis_size("sky"), lax.axis_size("band")
    cap = max(2, 2 * slots // sky)
    rows = side // nb
    single = sky > 4 or sky & (sky - 1) != 0
    tables = wave_tables(side, kernel_x.shape[1])
    sub, lane = tables["sub"], tables["lane"]
    chunk, partner, adds = band_plan(nb)
    near = 0 if single else min(2, sky)
    split = [True] if single else [r >= near for r in range(sky)]
    n_dest = sky if single else 1
    box = cap * rows
    out_shapes, first_out = [], []
    for cut in split:
        first_out.append(len(out_shapes))
        heights = [box + (HEAD if phase == 0 else 0) for phase in range(nb)] if cut else [nb * box + HEAD]
        out_shapes += [jax.ShapeDtypeStruct((n_dest, h, width), BF16) for h in heights]

    def place(outs, group, phase):
        return (outs[first_out[group] + phase], 0) if split[group] else (outs[first_out[group]], phase * box)

    def head(outs, group):
        return outs[first_out[group]], box if split[group] else nb * box

    plan = dict(sub=sub, lane=lane, rows=rows, nb=nb, scale=tables["scale"], slots=slots, cap=cap, sky=sky, per=PATCH_DEV,
                single=single, split=split, place=place, head=head, chunk=chunk, adds=adds)
    smem = pl.BlockSpec(memory_space=pltpu.SMEM)
    hbm = pl.BlockSpec(memory_space=pltpu.HBM)
    consts = [jnp.asarray(tables[n]) for n in ("to_col", "to_row", "from_col", "from_row", "tap_col", "tap_row")]
    args = [slot_owner.reshape(1, slots), slot_local, valid_rows, slot_visit, inv_var, basis_coef.transpose(1, 0, 2),
            kernel_x, kernel_y] + consts + [tiles]
    plan.update(n_in=len(args), n_out=len(out_shapes))
    landing = [pltpu.SMEM(a.shape, a.dtype) for a in args[:5]] + [pltpu.VMEM(a.shape, a.dtype) for a in args[5:]]
    sent = pl.pallas_call(
        functools.partial(convolve_kernel, plan),
        out_shape=out_shapes,
        in_specs=[hbm] * len(args),
        out_specs=[hbm] * len(out_shapes),
        scratch_shapes=landing + [
            pltpu.SemaphoreType.DMA((max(len(args) - 1 + slots, sky),)), pltpu.SemaphoreType.DMA((slots, nb)),
            pltpu.VMEM((2 * sub, kernel_x.shape[0]), F32),
            pltpu.VMEM((kernel_x.shape[0], 2 * lane), BF16), pltpu.VMEM((side, 2 * sub), BF16),
            pltpu.VMEM((sky, 1, 128), F32),
            pltpu.VMEM((slots, side, width), BF16), pltpu.VMEM((sky, HEAD, width), BF16)],
        compiler_params=pltpu.CompilerParams(vmem_limit_bytes=CONV_VMEM * MIB),
        cost_estimate=pl.CostEstimate(flops=slots * 22 * side**3, bytes_accessed=slots * side * side * 6,
                                      transcendentals=0),
        name="convolve",
    )(*args)

    swap = lambda a, r: a if r == 0 else lax.ppermute(a, "sky", [(i, i ^ r) for i in range(sky)])
    moved = list(sent)
    if single:
        moved = [lax.all_to_all(s, "sky", split_axis=0, concat_axis=0, tiled=True) for s in sent]
    else:
        for r in range(1, near):
            moved[first_out[r]] = swap(sent[first_out[r]], r)
        for phase in range(nb):
            for r in range(near, sky):
                moved[first_out[r] + phase] = swap(sent[first_out[r] + phase], r)

    band_buf, facts, arrived = None, None, []
    band_shape = jax.ShapeDtypeStruct((PATCH_DEV, side, width), F32)
    chunk_shape = (PATCH_DEV, rows, width)
    whole = lambda shape: pl.BlockSpec(shape, lambda *_: (0,) * len(shape))
    fact_shapes = [jax.ShapeDtypeStruct((sky, 128), jnp.int32), jax.ShapeDtypeStruct((sky, 128), F32)]
    for phase in range(nb):
        first, last = phase == 0, phase == nb - 1
        inputs, specs = [], []
        for group, cut in enumerate(split):
            inputs.append(place(moved, group, phase)[0])
            specs.append(pl.BlockSpec((n_dest, box, width), lambda i, at=0 if cut else phase: (0, at, 0)))
        for earlier in adds[phase]:
            inputs.append(arrived[earlier])
            specs.append(whole(chunk_shape))
        outs = [band_shape, jax.ShapeDtypeStruct(chunk_shape, F32 if last else BF16)]
        out_specs, aliases, scratch = [hbm, whole(chunk_shape)], {}, []
        if first:
            for group in range(len(split)):
                ref, start = head(moved, group)
                inputs.append(ref)
                specs.append(pl.BlockSpec((n_dest, HEAD, width), lambda i, at=start // HEAD: (0, at, 0)))
            outs, out_specs = outs + fact_shapes, out_specs + [smem] * 2
            scratch = [pltpu.VMEM(s.shape, s.dtype) for s in fact_shapes]
        else:
            inputs, specs = inputs + facts, specs + [smem] * 2
            aliases = {len(inputs): 0}
            inputs, specs = inputs + [band_buf], specs + [hbm]
        band_buf, extra, *rest = pl.pallas_call(
            functools.partial(sum_kernel, plan, phase),
            grid=(1,),
            out_shape=outs,
            in_specs=specs,
            out_specs=out_specs,
            scratch_shapes=[pltpu.VMEM(chunk_shape, F32), pltpu.VMEM((PATCH_DEV, rows, 128), F32),
                            pltpu.SemaphoreType.DMA((PATCH_DEV,))] + scratch,
            input_output_aliases=aliases,
            compiler_params=pltpu.CompilerParams(vmem_limit_bytes=SUM_VMEM * MIB),
            cost_estimate=pl.CostEstimate(flops=4 * PATCH_DEV * rows * width,
                                          bytes_accessed=12 * PATCH_DEV * rows * width, transcendentals=0),
            name="add_up",
        )(*inputs)
        facts = rest if first else facts
        if not last:
            arrived.append(lax.ppermute(extra, "band", [(b, partner(b, phase)) for b in range(nb)]))
    return (band_buf[None], extra)


def solution(mesh):
    in_specs = (
        P(("tract", "band"), "sky", None, None),
        P(("tract", "band"), "sky"),
        P(("tract", "band"), "sky", None),
        P(("tract", "band"), "sky"),
        P(("tract", "band"), "sky"),
        P(("tract", "band"), None, None),
        P(("tract", "band"), None),
        P(),
        P(),
    )
    out_specs = (P(("tract", "band"), "sky", None, None), P(("tract", "sky"), "band", None))
    return jax.shard_map(per_device, mesh=mesh, in_specs=in_specs, out_specs=out_specs, check_vma=False)
```

```python
import functools

import jax
import jax.numpy as jnp
import ml_dtypes
import numpy as np
from jax import lax
from jax.experimental import pallas as pl
from jax.experimental.pallas import tpu as pltpu
from jax.sharding import PartitionSpec as P

PATCH_DEV = 8
F32, BF16 = jnp.float32, jnp.bfloat16
MIB = 1024 * 1024
HEAD = 16
UNROLL = 4
LATE = 3
CONV_VMEM = 64
SUM_VMEM = 24


def round_up(value, multiple):
    return -(-value // multiple) * multiple


def wave_tables(side, kernel_len):
    half_len = kernel_len // 2
    count = -(-(side + half_len) // 2)
    omega = np.pi * (np.arange(count) + 0.5) / count
    sub, lane = round_up(count, 16), round_up(count, 128)

    def waves(points, width):
        out = np.zeros((len(points), 2 * width), np.float64)
        out[:, :count] = np.cos(np.outer(points, omega))
        out[:, width : width + count] = np.sin(np.outer(points, omega))
        return out

    pixels, taps = np.arange(side), np.arange(kernel_len) - half_len
    held = lambda a: np.ascontiguousarray(a).astype(ml_dtypes.bfloat16)
    return dict(
        sub=sub,
        lane=lane,
        scale=1.0 / (count * count),
        to_col=held(waves(pixels, lane)),
        to_row=held(waves(pixels, sub).T),
        from_col=held(waves(pixels, lane).T),
        from_row=held(waves(pixels, sub)),
        tap_col=held(waves(taps, lane)),
        tap_row=held(waves(taps, sub).T),
    )


def dot(a, b, contract=((1,), (0,))):
    return lax.dot_general(a, b, (contract, ((), ())), preferred_element_type=F32)


def weigh(rows, tables):
    lane = rows[0].shape[1] // 2
    (c, s), (tc, ts) = rows, tables
    cc, cs, sc, ss = c[:, :lane], c[:, lane:], s[:, :lane], s[:, lane:]
    pa, pb, qa, qb = tc[:, :lane], tc[:, lane:], ts[:, :lane], ts[:, lane:]
    return (
        (pa * cc + pb * cs + qa * sc + qb * ss).astype(BF16),
        (pa * cs - pb * cc + qa * ss - qb * sc).astype(BF16),
        (pa * sc + pb * ss - qa * cc - qb * cs).astype(BF16),
        (pa * ss - pb * sc - qa * cs + qb * cc).astype(BF16),
    )


def convolve_kernel(plan, *refs):
    n_in, n_out = plan["n_in"], plan["n_out"]
    sources, outs, held = refs[:n_in], refs[n_in : n_in + n_out], refs[n_in + n_out :]
    local, (sems, out_sems, row_waves, col_waves, back, heads, done, head_rows) = held[:n_in], held[n_in:]
    sub, lane, rows, nb, cap, slots = (plan[k] for k in ("sub", "lane", "rows", "nb", "cap", "slots"))
    copies = [pltpu.make_async_copy(a, b, sems.at[i]) for i, (a, b) in enumerate(zip(sources[:-1], local[:-1]))]
    tiles = [
        pltpu.make_async_copy(sources[-1].at[s], local[-1].at[s], sems.at[n_in - 1 + s]) for s in range(slots)
    ]
    for copy in copies + tiles:
        copy.start()
    owner, local_id, valid, visit, inv_var, coef, kx, ky, to_col, to_row, from_col, from_row, tap_col, tap_row, patch = local
    for copy in copies:
        copy.wait()
    side = patch.shape[1]
    row_waves[...] = dot(tap_row[...], ky[...], ((1,), (1,)))
    col_waves[...] = (dot(kx[...], tap_col[...]) * plan["scale"]).astype(BF16)
    band = lax.axis_index("band")
    for phase in range(nb):
        start = pl.multiple_of(plan["chunk"](band, phase) * rows, rows)
        back[phase * rows : (phase + 1) * rows, :] = from_row[pl.ds(start, rows), :]
    heads[...] = jnp.full(heads.shape, -1.0, F32)
    me = lax.axis_index("sky")
    basis = kx.shape[0]
    lanes = lax.broadcasted_iota(jnp.int32, (1, 128), 1)

    def convolved(slot):
        seen = visit[0, slot]
        weight = jnp.full((1, basis), inv_var[0, seen], F32).astype(BF16).astype(F32)
        mixing = (weight * coef[seen].astype(BF16).astype(F32)).astype(BF16).astype(F32)
        row_ids = lax.broadcasted_iota(jnp.int32, (side, side), 0)
        masked = jnp.where(row_ids < valid[0, slot], patch[slot], 0.0).astype(BF16)
        col = dot(masked, to_col[...]).astype(BF16)
        mixed = (row_waves[...] * mixing).astype(BF16)
        parts = (dot(to_row[:sub, :], col), dot(to_row[sub:, :], col))
        tables = (dot(mixed[:sub], col_waves[...]), dot(mixed[sub:], col_waves[...]))
        y_cc, y_cs, y_sc, y_ss = weigh(parts, tables)
        z_c = dot(y_cc, from_col[:lane, :]) + dot(y_cs, from_col[lane:, :])
        z_s = dot(y_sc, from_col[:lane, :]) + dot(y_ss, from_col[lane:, :])
        return (dot(back[:, :sub], z_c.astype(BF16)) + dot(back[:, sub:], z_s.astype(BF16))).astype(BF16)

    def sent(slot, phase, ref):
        return pltpu.make_async_copy(done.at[slot, phase * rows : (phase + 1) * rows, :], ref, out_sems.at[slot, phase])

    def deliver(slot, full):
        done[slot] = full
        mine = owner[0, slot]
        rank = jnp.int32(0)
        for other in range(slots):
            rank = rank + jnp.where((other < slot) & (owner[0, other] == mine), 1, 0).astype(jnp.int32)
        box = mine if plan["single"] else mine ^ me
        weight = jnp.full((1, 128), inv_var[0, visit[0, slot]], F32)
        facts = jnp.where(lanes == 8 * rank, local_id[0, slot].astype(F32), heads[box])
        facts = jnp.where(lanes == 8 * rank + 1, valid[0, slot].astype(F32), facts)
        heads[box] = jnp.where(lanes == 8 * rank + 2, weight, facts)
        def store(box):
            for phase in range(nb):
                ref, at, first = plan["place"](outs, box, phase)
                start = pl.multiple_of(first + rank * rows, rows)
                sent(slot, phase, ref.at[at, pl.ds(start, rows), :]).start()

        if plan["single"]:
            store(mine)
        else:
            for index in range(plan["sky"]):
                pl.when(box == index)(functools.partial(store, index))

    def some(step, carry):
        slots_now = [step * UNROLL + u for u in range(UNROLL)]
        for s in slots_now:
            pltpu.make_async_copy(sources[-1].at[s], local[-1].at[s], sems.at[n_in - 1 + s]).wait()
        results = [convolved(s) for s in slots_now]
        for s, full in zip(slots_now, results):
            deliver(s, full)
        return carry

    lax.fori_loop(0, slots // UNROLL, some, 0)
    width = patch.shape[2]
    copies = []
    for index in range(plan["sky"]):
        ref, at, first = plan["head"](outs, index)
        row = jnp.concatenate([heads[index]] * (width // 128), axis=1)
        head_rows[index] = jnp.broadcast_to(row, (HEAD, width)).astype(BF16)
        copies.append(pltpu.make_async_copy(head_rows.at[index], ref.at[at, first : first + HEAD, :], sems.at[index]))
        copies[-1].start()
    for copy in copies:
        copy.wait()
    for slot in range(slots):
        for phase in range(nb):
            sent(slot, phase, plan["place"](outs, 0, phase)[0].at[0, 0:rows, :]).wait()


def sum_kernel(plan, phase, *refs):
    sky, nb, rows, cap, per = plan["sky"], plan["nb"], plan["rows"], plan["cap"], plan["per"]
    first, last = phase == 0, phase == nb - 1
    refs = list(refs)
    take = lambda n: [refs.pop(0) for _ in range(n)]
    boxes = take(plan["n_boxes"])
    arrived = take(len(plan["adds"][phase]))
    heads = take(plan["n_boxes"]) if first else None
    facts = None if first else take(2)
    if not first:
        take(1)
    band_out, extra = take(2)
    if first:
        facts = take(2)
    acc, cov, sems = take(3)
    if first:
        whole_facts, weights = take(2)
        rows_of = [h[d, 0:1, :128].astype(F32) for h in heads for d in range(h.shape[0])]
        for source, row in enumerate(rows_of):
            whole_facts[source : source + 1, :] = row.astype(jnp.int32)
            weights[source : source + 1, :] = row
        copies = [pltpu.make_async_copy(a, b, sems.at[i]) for i, (a, b) in enumerate(((whole_facts, facts[0]), (weights, facts[1])))]
        for copy in copies:
            copy.start()
    chunk = plan["chunk"](lax.axis_index("band"), phase)
    acc[...] = jnp.zeros_like(acc)
    cov[...] = jnp.zeros_like(cov)
    row_ids = chunk * rows + lax.broadcasted_iota(jnp.int32, (rows, 128), 0)
    if first:
        for copy in copies:
            copy.wait()
    for source in range(sky):
        group, at = (0, source) if plan["single"] else (source, 0)
        for rank in range(cap):
            local = facts[0][source, 8 * rank]

            @pl.when(local >= 0)
            def _(group=group, at=at, rank=rank, source=source, local=local):
                acc[local] += boxes[group][at, rank * rows : (rank + 1) * rows, :].astype(F32)
                weight = jnp.full((rows, 128), facts[1][source, 8 * rank + 2], F32)
                cov[local] += jnp.where(row_ids < facts[0][source, 8 * rank + 1], weight, 0.0)

    width = acc.shape[2]
    copies = []
    for patch in range(per):
        factor = 1.0 / jnp.maximum(cov[patch], 1.0)
        for at in range(0, width, 128):
            value = acc[patch, :, at : at + 128] * factor
            acc[patch, :, at : at + 128] = value
            for other in arrived:
                value = value + other[patch, :, at : at + 128].astype(F32)
            extra[patch, :, at : at + 128] = value.astype(extra.dtype)
        copies.append(pltpu.make_async_copy(
            acc.at[patch], band_out.at[patch, pl.ds(pl.multiple_of(chunk * rows, rows), rows), :], sems.at[patch]))
        copies[-1].start()
    for copy in copies:
        copy.wait()


def band_plan(nb):
    if nb & (nb - 1) == 0:
        masks = sorted(range(1, nb), key=lambda m: (-m.bit_length(), m)) + [0]
        return lambda band, phase: band ^ masks[phase]
    shifts = sorted(range(1, nb), key=lambda k: -min(k, nb - k)) + [0]
    return lambda band, phase: (
        (band + shifts[phase]) % nb if isinstance(band, int) else lax.rem(band + shifts[phase], nb)
    )


def accumulate_kernel(*refs):
    total, *terms, out = refs
    value = total[...]
    for term in terms:
        value = value + term[...].astype(F32)
    out[...] = value


def per_device(patches, valid_rows, slot_owner, slot_local, slot_visit, basis_coef, inv_var, kernel_x, kernel_y):
    tiles = patches[0]
    slots, side, width = tiles.shape
    sky, nb = lax.axis_size("sky"), lax.axis_size("band")
    cap = max(2, 2 * slots // sky)
    rows = side // nb
    single = sky != 4
    tables = wave_tables(side, kernel_x.shape[1])
    sub, lane = tables["sub"], tables["lane"]
    chunk = band_plan(nb)
    late = min(LATE, nb - 1)
    adds = [[]] * (nb - 1) + [list(range(nb - 1 - late))]
    box = cap * rows
    shaped = lambda count, height: jax.ShapeDtypeStruct((count, height, width), BF16)
    if single:
        out_shapes = [shaped(sky, box + (HEAD if phase == 0 else 0)) for phase in range(nb)]
        place = lambda outs, dest, phase: (outs[phase], dest, 0)
        head = lambda outs, dest: (outs[0], dest, box)
    else:
        cut = lambda phase: shaped(1, box + (HEAD if phase == 0 else 0))
        out_shapes = [shaped(1, nb * box + HEAD)] + [cut(phase) for phase in range(nb) for _ in range(3)]

        def place(outs, dest, phase):
            if dest == 1:
                return outs[0], 0, phase * box
            return outs[1 + 3 * phase + max(0, dest - 1)], 0, 0

        def head(outs, dest):
            return place(outs, dest, 0)[0], 0, nb * box if dest == 1 else box

    plan = dict(sub=sub, lane=lane, rows=rows, nb=nb, scale=tables["scale"], slots=slots, cap=cap, sky=sky, per=PATCH_DEV,
                single=single, n_boxes=1 if single else sky, place=place, head=head, chunk=chunk, adds=adds)
    smem = pl.BlockSpec(memory_space=pltpu.SMEM)
    hbm = pl.BlockSpec(memory_space=pltpu.HBM)
    consts = [jnp.asarray(tables[n]) for n in ("to_col", "to_row", "from_col", "from_row", "tap_col", "tap_row")]
    args = [slot_owner.reshape(1, slots), slot_local, valid_rows, slot_visit, inv_var, basis_coef.transpose(1, 0, 2),
            kernel_x, kernel_y] + consts + [tiles]
    plan.update(n_in=len(args), n_out=len(out_shapes))
    landing = [pltpu.SMEM(a.shape, a.dtype) for a in args[:5]] + [pltpu.VMEM(a.shape, a.dtype) for a in args[5:]]
    sent = pl.pallas_call(
        functools.partial(convolve_kernel, plan),
        out_shape=out_shapes,
        in_specs=[hbm] * len(args),
        out_specs=[hbm] * len(out_shapes),
        scratch_shapes=landing + [
            pltpu.SemaphoreType.DMA((max(len(args) - 1 + slots, sky),)), pltpu.SemaphoreType.DMA((slots, nb)),
            pltpu.VMEM((2 * sub, kernel_x.shape[0]), F32),
            pltpu.VMEM((kernel_x.shape[0], 2 * lane), BF16), pltpu.VMEM((side, 2 * sub), BF16),
            pltpu.VMEM((sky, 1, 128), F32),
            pltpu.VMEM((slots, side, width), BF16), pltpu.VMEM((sky, HEAD, width), BF16)],
        compiler_params=pltpu.CompilerParams(vmem_limit_bytes=CONV_VMEM * MIB),
        cost_estimate=pl.CostEstimate(flops=slots * 22 * side**3, bytes_accessed=slots * side * side * 6,
                                      transcendentals=0),
        name="convolve",
    )(*args)

    swap = lambda a, r: a if r == 0 else lax.ppermute(a, "sky", [(i, i ^ r) for i in range(sky)])
    if single:
        moved = [lax.all_to_all(s, "sky", split_axis=0, concat_axis=0, tiled=True) for s in sent]
        pieces = lambda phase: [(moved[phase], sky, 0, 0, box)]
    else:
        near = swap(sent[0], 1)
        cuts = [swap(a, (0, 2, 3)[i % 3]) for i, a in enumerate(sent[1:])]

        def pieces(phase):
            mine, *others = cuts[3 * phase : 3 * phase + 3]
            return [(mine, 1, 0, 0, box), (near, 1, 0, phase, nb * box)] + [(a, 1, 0, 0, box) for a in others]

    band_buf, facts, arrived = None, None, []
    band_shape = jax.ShapeDtypeStruct((PATCH_DEV, side, width), F32)
    chunk_shape = (PATCH_DEV, rows, width)
    whole = lambda shape: pl.BlockSpec(shape, lambda *_: (0,) * len(shape))
    fact_shapes = [jax.ShapeDtypeStruct((sky, 128), jnp.int32), jax.ShapeDtypeStruct((sky, 128), F32)]
    for phase in range(nb):
        first, last = phase == 0, phase == nb - 1
        inputs, specs = [], []
        for array, count, at, row, _ in pieces(phase):
            inputs.append(array)
            specs.append(pl.BlockSpec((count, box, width), lambda i, at=at, row=row: (at, row, 0)))
        for earlier in adds[phase]:
            inputs.append(arrived[earlier])
            specs.append(whole(chunk_shape))
        outs = [band_shape, jax.ShapeDtypeStruct(chunk_shape, F32 if last else BF16)]
        out_specs, aliases, scratch = [hbm, whole(chunk_shape)], {}, []
        if first:
            for array, count, at, _, end in pieces(phase):
                inputs.append(array)
                specs.append(pl.BlockSpec((count, HEAD, width), lambda i, at=at, end=end: (at, end // HEAD, 0)))
            outs, out_specs = outs + fact_shapes, out_specs + [smem] * 2
            scratch = [pltpu.VMEM(s.shape, s.dtype) for s in fact_shapes]
        else:
            inputs, specs = inputs + facts, specs + [smem] * 2
            aliases = {len(inputs): 0}
            inputs, specs = inputs + [band_buf], specs + [hbm]
        band_buf, extra, *rest = pl.pallas_call(
            functools.partial(sum_kernel, plan, phase),
            grid=(1,),
            out_shape=outs,
            in_specs=specs,
            out_specs=out_specs,
            scratch_shapes=[pltpu.VMEM(chunk_shape, F32), pltpu.VMEM((PATCH_DEV, rows, 128), F32),
                            pltpu.SemaphoreType.DMA((PATCH_DEV,))] + scratch,
            input_output_aliases=aliases,
            compiler_params=pltpu.CompilerParams(vmem_limit_bytes=SUM_VMEM * MIB),
            cost_estimate=pl.CostEstimate(flops=4 * PATCH_DEV * rows * width,
                                          bytes_accessed=12 * PATCH_DEV * rows * width, transcendentals=0),
            name="add_up",
        )(*inputs)
        facts = rest if first else facts
        if not last:
            arrived.append(lax.ppermute(extra, "band", [(b, chunk(b, phase)) for b in range(nb)]))
    if late:
        terms = arrived[nb - 1 - late :]
        for i in range(late - 1):
            extra, terms[i] = lax.optimization_barrier((extra, terms[i]))
        extra = pl.pallas_call(
            accumulate_kernel, grid=(1,), out_shape=jax.ShapeDtypeStruct(chunk_shape, F32),
            in_specs=[whole(chunk_shape)] * (1 + late), out_specs=whole(chunk_shape), input_output_aliases={0: 0},
            compiler_params=pltpu.CompilerParams(vmem_limit_bytes=SUM_VMEM * MIB), name="accumulate",
        )(extra, *terms)
    return (band_buf[None], extra)


def solution(mesh):
    in_specs = (
        P(("tract", "band"), "sky", None, None),
        P(("tract", "band"), "sky"),
        P(("tract", "band"), "sky", None),
        P(("tract", "band"), "sky"),
        P(("tract", "band"), "sky"),
        P(("tract", "band"), None, None),
        P(("tract", "band"), None),
        P(),
        P(),
    )
    out_specs = (P(("tract", "band"), "sky", None, None), P(("tract", "sky"), "band", None))
    return jax.shard_map(per_device, mesh=mesh, in_specs=in_specs, out_specs=out_specs, check_vma=False)
```

```python
import functools

import jax
import jax.numpy as jnp
import ml_dtypes
import numpy as np
from jax import lax
from jax.experimental import pallas as pl
from jax.experimental.pallas import tpu as pltpu
from jax.sharding import PartitionSpec as P

PATCH_DEV = 8
F32, BF16 = jnp.float32, jnp.bfloat16
MIB = 1024 * 1024
HEAD = 16
UNROLL = 8
LATE = 3
CONV_VMEM = 64
SUM_VMEM = 24


def round_up(value, multiple):
    return -(-value // multiple) * multiple


def wave_tables(side, kernel_len):
    half_len = kernel_len // 2
    count = -(-(side + half_len) // 2)
    omega = np.pi * (np.arange(count) + 0.5) / count
    sub, lane = round_up(count, 16), round_up(count, 128)

    def waves(points, width):
        out = np.zeros((len(points), 2 * width), np.float64)
        out[:, :count] = np.cos(np.outer(points, omega))
        out[:, width : width + count] = np.sin(np.outer(points, omega))
        return out

    pixels, taps = np.arange(side), np.arange(kernel_len) - half_len
    held = lambda a: np.ascontiguousarray(a).astype(ml_dtypes.bfloat16)
    return dict(
        sub=sub,
        lane=lane,
        scale=1.0 / (count * count),
        to_col=held(waves(pixels, lane)),
        to_row=held(waves(pixels, sub).T),
        from_col=held(waves(pixels, lane).T),
        from_row=held(waves(pixels, sub)),
        tap_col=held(waves(taps, lane)),
        tap_row=held(waves(taps, sub).T),
    )


def dot(a, b, contract=((1,), (0,))):
    return lax.dot_general(a, b, (contract, ((), ())), preferred_element_type=F32)


def weigh(rows, tables):
    lane = rows[0].shape[1] // 2
    (c, s), (tc, ts) = rows, tables
    cc, cs, sc, ss = c[:, :lane], c[:, lane:], s[:, :lane], s[:, lane:]
    pa, pb, qa, qb = tc[:, :lane], tc[:, lane:], ts[:, :lane], ts[:, lane:]
    return (
        (pa * cc + pb * cs + qa * sc + qb * ss).astype(BF16),
        (pa * cs - pb * cc + qa * ss - qb * sc).astype(BF16),
        (pa * sc + pb * ss - qa * cc - qb * cs).astype(BF16),
        (pa * ss - pb * sc - qa * cs + qb * cc).astype(BF16),
    )


def convolve_kernel(plan, *refs):
    n_in, n_out = plan["n_in"], plan["n_out"]
    sources, outs, held = refs[:n_in], refs[n_in : n_in + n_out], refs[n_in + n_out :]
    local, (sems, out_sems, row_waves, col_waves, back, heads, done, head_rows) = held[:n_in], held[n_in:]
    sub, lane, rows, nb, cap, slots = (plan[k] for k in ("sub", "lane", "rows", "nb", "cap", "slots"))
    copies = [pltpu.make_async_copy(a, b, sems.at[i]) for i, (a, b) in enumerate(zip(sources[:-1], local[:-1]))]
    tiles = [
        pltpu.make_async_copy(sources[-1].at[s], local[-1].at[s], sems.at[n_in - 1 + s]) for s in range(slots)
    ]
    for copy in copies + tiles:
        copy.start()
    owner, local_id, valid, visit, inv_var, coef, kx, ky, to_col, to_row, from_col, from_row, tap_col, tap_row, patch = local
    for copy in copies:
        copy.wait()
    side = patch.shape[1]
    row_waves[...] = dot(tap_row[...], ky[...], ((1,), (1,)))
    col_waves[...] = (dot(kx[...], tap_col[...]) * plan["scale"]).astype(BF16)
    band = lax.axis_index("band")
    for phase in range(nb):
        start = pl.multiple_of(plan["chunk"](band, phase) * rows, rows)
        back[phase * rows : (phase + 1) * rows, :] = from_row[pl.ds(start, rows), :]
    heads[...] = jnp.full(heads.shape, -1.0, F32)
    me = lax.axis_index("sky")
    basis = kx.shape[0]
    lanes = lax.broadcasted_iota(jnp.int32, (1, 128), 1)

    def convolved(slot):
        seen = visit[0, slot]
        weight = jnp.full((1, basis), inv_var[0, seen], F32).astype(BF16).astype(F32)
        mixing = (weight * coef[seen].astype(BF16).astype(F32)).astype(BF16).astype(F32)
        row_ids = lax.broadcasted_iota(jnp.int32, (side, side), 0)
        masked = jnp.where(row_ids < valid[0, slot], patch[slot], 0.0).astype(BF16)
        col = dot(masked, to_col[...]).astype(BF16)
        mixed = (row_waves[...] * mixing).astype(BF16)
        parts = (dot(to_row[:sub, :], col), dot(to_row[sub:, :], col))
        tables = (dot(mixed[:sub], col_waves[...]), dot(mixed[sub:], col_waves[...]))
        y_cc, y_cs, y_sc, y_ss = weigh(parts, tables)
        z_c = dot(y_cc, from_col[:lane, :]) + dot(y_cs, from_col[lane:, :])
        z_s = dot(y_sc, from_col[:lane, :]) + dot(y_ss, from_col[lane:, :])
        return (dot(back[:, :sub], z_c.astype(BF16)) + dot(back[:, sub:], z_s.astype(BF16))).astype(BF16)

    def sent(slot, phase, ref):
        return pltpu.make_async_copy(done.at[slot, phase * rows : (phase + 1) * rows, :], ref, out_sems.at[slot, phase])

    def deliver(slot, full):
        done[slot] = full
        mine = owner[0, slot]
        rank = jnp.int32(0)
        for other in range(slots):
            rank = rank + jnp.where((other < slot) & (owner[0, other] == mine), 1, 0).astype(jnp.int32)
        box = mine if plan["single"] else mine ^ me
        weight = jnp.full((1, 128), inv_var[0, visit[0, slot]], F32)
        facts = jnp.where(lanes == 8 * rank, local_id[0, slot].astype(F32), heads[box])
        facts = jnp.where(lanes == 8 * rank + 1, valid[0, slot].astype(F32), facts)
        heads[box] = jnp.where(lanes == 8 * rank + 2, weight, facts)
        def store(box):
            for phase in range(nb):
                ref, at, first = plan["place"](outs, box, phase)
                start = pl.multiple_of(first + rank * rows, rows)
                sent(slot, phase, ref.at[at, pl.ds(start, rows), :]).start()

        if plan["single"]:
            store(mine)
        else:
            for index in range(plan["sky"]):
                pl.when(box == index)(functools.partial(store, index))

    def some(step, carry):
        slots_now = [step * UNROLL + u for u in range(min(UNROLL, slots))]
        for s in slots_now:
            pltpu.make_async_copy(sources[-1].at[s], local[-1].at[s], sems.at[n_in - 1 + s]).wait()
        results = [convolved(s) for s in slots_now]
        for s, full in zip(slots_now, results):
            deliver(s, full)
        return carry

    lax.fori_loop(0, max(1, slots // UNROLL), some, 0)
    width = patch.shape[2]
    copies = []
    for index in range(plan["sky"]):
        ref, at, first = plan["head"](outs, index)
        row = jnp.concatenate([heads[index]] * (width // 128), axis=1)
        head_rows[index] = jnp.broadcast_to(row, (HEAD, width)).astype(BF16)
        copies.append(pltpu.make_async_copy(head_rows.at[index], ref.at[at, first : first + HEAD, :], sems.at[index]))
        copies[-1].start()
    for copy in copies:
        copy.wait()
    for slot in range(slots):
        for phase in range(nb):
            sent(slot, phase, plan["place"](outs, 0, phase)[0].at[0, 0:rows, :]).wait()


def sum_kernel(plan, phase, *refs):
    sky, nb, rows, cap, per = plan["sky"], plan["nb"], plan["rows"], plan["cap"], plan["per"]
    first, last = phase == 0, phase == nb - 1
    refs = list(refs)
    take = lambda n: [refs.pop(0) for _ in range(n)]
    boxes = take(plan["n_boxes"])
    arrived = take(len(plan["adds"][phase]))
    heads = take(plan["n_boxes"]) if first else None
    facts = None if first else take(2)
    if not first:
        take(1)
    band_out, extra = take(2)
    if first:
        facts = take(2)
    acc, cov, sems = take(3)
    if first:
        whole_facts, weights = take(2)
        rows_of = [h[d, 0:1, :128].astype(F32) for h in heads for d in range(h.shape[0])]
        for source, row in enumerate(rows_of):
            whole_facts[source : source + 1, :] = row.astype(jnp.int32)
            weights[source : source + 1, :] = row
        copies = [pltpu.make_async_copy(a, b, sems.at[i]) for i, (a, b) in enumerate(((whole_facts, facts[0]), (weights, facts[1])))]
        for copy in copies:
            copy.start()
    chunk = plan["chunk"](lax.axis_index("band"), phase)
    acc[...] = jnp.zeros_like(acc)
    cov[...] = jnp.zeros_like(cov)
    row_ids = chunk * rows + lax.broadcasted_iota(jnp.int32, (rows, 128), 0)
    if first:
        for copy in copies:
            copy.wait()
    for source in range(sky):
        group, at = (0, source) if plan["single"] else (source, 0)
        for rank in range(cap):
            local = facts[0][source, 8 * rank]

            @pl.when(local >= 0)
            def _(group=group, at=at, rank=rank, source=source, local=local):
                acc[local] += boxes[group][at, rank * rows : (rank + 1) * rows, :].astype(F32)
                weight = jnp.full((rows, 128), facts[1][source, 8 * rank + 2], F32)
                cov[local] += jnp.where(row_ids < facts[0][source, 8 * rank + 1], weight, 0.0)

    width = acc.shape[2]
    copies = []
    for patch in range(per):
        factor = 1.0 / jnp.maximum(cov[patch], 1.0)
        for at in range(0, width, 128):
            value = acc[patch, :, at : at + 128] * factor
            acc[patch, :, at : at + 128] = value
            for other in arrived:
                value = value + other[patch, :, at : at + 128].astype(F32)
            extra[patch, :, at : at + 128] = value.astype(extra.dtype)
        copies.append(pltpu.make_async_copy(
            acc.at[patch], band_out.at[patch, pl.ds(pl.multiple_of(chunk * rows, rows), rows), :], sems.at[patch]))
        copies[-1].start()
    for copy in copies:
        copy.wait()


def band_plan(nb):
    shifts = list(range(1, nb)) + [0]
    return lambda band, phase: (
        (band + shifts[phase]) % nb if isinstance(band, int) else lax.rem(band + shifts[phase], nb)
    )


def accumulate_kernel(*refs):
    total, *terms, out = refs
    value = total[...]
    for term in terms:
        value = value + term[...].astype(F32)
    out[...] = value


def per_device(patches, valid_rows, slot_owner, slot_local, slot_visit, basis_coef, inv_var, kernel_x, kernel_y):
    tiles = patches[0]
    slots, side, width = tiles.shape
    sky, nb = lax.axis_size("sky"), lax.axis_size("band")
    cap = max(2, 2 * slots // sky)
    rows = side // nb
    single = sky != 4
    tables = wave_tables(side, kernel_x.shape[1])
    sub, lane = tables["sub"], tables["lane"]
    chunk = band_plan(nb)
    late = min(LATE, nb - 1)
    adds = [[]] * (nb - 1) + [list(range(nb - 1 - late))]
    box = cap * rows
    shaped = lambda count, height: jax.ShapeDtypeStruct((count, height, width), BF16)
    if single:
        out_shapes = [shaped(sky, box + (HEAD if phase == 0 else 0)) for phase in range(nb)]
        place = lambda outs, dest, phase: (outs[phase], dest, 0)
        head = lambda outs, dest: (outs[0], dest, box)
    else:
        cut = lambda phase: shaped(1, box + (HEAD if phase == 0 else 0))
        out_shapes = [shaped(1, nb * box + HEAD)] + [cut(phase) for phase in range(nb) for _ in range(3)]

        def place(outs, dest, phase):
            if dest == 1:
                return outs[0], 0, phase * box
            return outs[1 + 3 * phase + max(0, dest - 1)], 0, 0

        def head(outs, dest):
            return place(outs, dest, 0)[0], 0, nb * box if dest == 1 else box

    plan = dict(sub=sub, lane=lane, rows=rows, nb=nb, scale=tables["scale"], slots=slots, cap=cap, sky=sky, per=PATCH_DEV,
                single=single, n_boxes=1 if single else sky, place=place, head=head, chunk=chunk, adds=adds)
    smem = pl.BlockSpec(memory_space=pltpu.SMEM)
    hbm = pl.BlockSpec(memory_space=pltpu.HBM)
    consts = [jnp.asarray(tables[n]) for n in ("to_col", "to_row", "from_col", "from_row", "tap_col", "tap_row")]
    args = [slot_owner.reshape(1, slots), slot_local, valid_rows, slot_visit, inv_var, basis_coef.transpose(1, 0, 2),
            kernel_x, kernel_y] + consts + [tiles]
    plan.update(n_in=len(args), n_out=len(out_shapes))
    landing = [pltpu.SMEM(a.shape, a.dtype) for a in args[:5]] + [pltpu.VMEM(a.shape, a.dtype) for a in args[5:]]
    sent = pl.pallas_call(
        functools.partial(convolve_kernel, plan),
        out_shape=out_shapes,
        in_specs=[hbm] * len(args),
        out_specs=[hbm] * len(out_shapes),
        scratch_shapes=landing + [
            pltpu.SemaphoreType.DMA((max(len(args) - 1 + slots, sky),)), pltpu.SemaphoreType.DMA((slots, nb)),
            pltpu.VMEM((2 * sub, kernel_x.shape[0]), F32),
            pltpu.VMEM((kernel_x.shape[0], 2 * lane), BF16), pltpu.VMEM((side, 2 * sub), BF16),
            pltpu.VMEM((sky, 1, 128), F32),
            pltpu.VMEM((slots, side, width), BF16), pltpu.VMEM((sky, HEAD, width), BF16)],
        compiler_params=pltpu.CompilerParams(vmem_limit_bytes=CONV_VMEM * MIB),
        cost_estimate=pl.CostEstimate(flops=slots * 22 * side**3, bytes_accessed=slots * side * side * 6,
                                      transcendentals=0),
        name="convolve",
    )(*args)

    swap = lambda a, r: a if r == 0 else lax.ppermute(a, "sky", [(i, i ^ r) for i in range(sky)])
    if single:
        moved = [lax.all_to_all(s, "sky", split_axis=0, concat_axis=0, tiled=True) for s in sent]
        pieces = lambda phase: [(moved[phase], sky, 0, 0, box)]
    else:
        near = swap(sent[0], 1)
        cuts = [swap(a, (0, 2, 3)[i % 3]) for i, a in enumerate(sent[1:])]

        def pieces(phase):
            mine, *others = cuts[3 * phase : 3 * phase + 3]
            return [(mine, 1, 0, 0, box), (near, 1, 0, phase, nb * box)] + [(a, 1, 0, 0, box) for a in others]

    band_buf, facts, arrived = None, None, []
    band_shape = jax.ShapeDtypeStruct((PATCH_DEV, side, width), F32)
    chunk_shape = (PATCH_DEV, rows, width)
    whole = lambda shape: pl.BlockSpec(shape, lambda *_: (0,) * len(shape))
    fact_shapes = [jax.ShapeDtypeStruct((sky, 128), jnp.int32), jax.ShapeDtypeStruct((sky, 128), F32)]
    for phase in range(nb):
        first, last = phase == 0, phase == nb - 1
        inputs, specs = [], []
        for array, count, at, row, _ in pieces(phase):
            inputs.append(array)
            specs.append(pl.BlockSpec((count, box, width), lambda i, at=at, row=row: (at, row, 0)))
        for earlier in adds[phase]:
            inputs.append(arrived[earlier])
            specs.append(whole(chunk_shape))
        outs = [band_shape, jax.ShapeDtypeStruct(chunk_shape, F32 if last else BF16)]
        out_specs, aliases, scratch = [hbm, whole(chunk_shape)], {}, []
        if first:
            for array, count, at, _, end in pieces(phase):
                inputs.append(array)
                specs.append(pl.BlockSpec((count, HEAD, width), lambda i, at=at, end=end: (at, end // HEAD, 0)))
            outs, out_specs = outs + fact_shapes, out_specs + [smem] * 2
            scratch = [pltpu.VMEM(s.shape, s.dtype) for s in fact_shapes]
        else:
            inputs, specs = inputs + facts, specs + [smem] * 2
            aliases = {len(inputs): 0}
            inputs, specs = inputs + [band_buf], specs + [hbm]
        band_buf, extra, *rest = pl.pallas_call(
            functools.partial(sum_kernel, plan, phase),
            grid=(1,),
            out_shape=outs,
            in_specs=specs,
            out_specs=out_specs,
            scratch_shapes=[pltpu.VMEM(chunk_shape, F32), pltpu.VMEM((PATCH_DEV, rows, 128), F32),
                            pltpu.SemaphoreType.DMA((PATCH_DEV,))] + scratch,
            input_output_aliases=aliases,
            compiler_params=pltpu.CompilerParams(vmem_limit_bytes=SUM_VMEM * MIB),
            cost_estimate=pl.CostEstimate(flops=4 * PATCH_DEV * rows * width,
                                          bytes_accessed=12 * PATCH_DEV * rows * width, transcendentals=0),
            name="add_up",
        )(*inputs)
        facts = rest if first else facts
        if not last:
            arrived.append(lax.ppermute(extra, "band", [(b, chunk(b, phase)) for b in range(nb)]))
    if late:
        terms = arrived[nb - 1 - late :]
        for i in range(late - 1):
            extra, terms[i] = lax.optimization_barrier((extra, terms[i]))
        extra = pl.pallas_call(
            accumulate_kernel, grid=(1,), out_shape=jax.ShapeDtypeStruct(chunk_shape, F32),
            in_specs=[whole(chunk_shape)] * (1 + late), out_specs=whole(chunk_shape), input_output_aliases={0: 0},
            compiler_params=pltpu.CompilerParams(vmem_limit_bytes=SUM_VMEM * MIB), name="accumulate",
        )(extra, *terms)
    return (band_buf[None], extra)


def solution(mesh):
    in_specs = (
        P(("tract", "band"), "sky", None, None),
        P(("tract", "band"), "sky"),
        P(("tract", "band"), "sky", None),
        P(("tract", "band"), "sky"),
        P(("tract", "band"), "sky"),
        P(("tract", "band"), None, None),
        P(("tract", "band"), None),
        P(),
        P(),
    )
    out_specs = (P(("tract", "band"), "sky", None, None), P(("tract", "sky"), "band", None))
    return jax.shard_map(per_device, mesh=mesh, in_specs=in_specs, out_specs=out_specs, check_vma=False)
```

```python
import functools

import jax
import jax.numpy as jnp
import ml_dtypes
import numpy as np
from jax import lax
from jax.experimental import pallas as pl
from jax.experimental.pallas import tpu as pltpu
from jax.sharding import PartitionSpec as P

PATCH_DEV = 8
F32, BF16 = jnp.float32, jnp.bfloat16
MIB = 1024 * 1024
HEAD = 16
STAGE = True
BATCH = 4
CONV_VMEM = 64
SUM_VMEM = 24


def round_up(value, multiple):
    return -(-value // multiple) * multiple


def wave_tables(side, kernel_len):
    half_len = kernel_len // 2
    count = -(-(side + half_len) // 2)
    omega = np.pi * (np.arange(count) + 0.5) / count
    sub, lane = round_up(count, 16), round_up(count, 128)

    def waves(points, width):
        out = np.zeros((len(points), 2 * width), np.float64)
        out[:, :count] = np.cos(np.outer(points, omega))
        out[:, width : width + count] = np.sin(np.outer(points, omega))
        return out

    pixels, taps = np.arange(side), np.arange(kernel_len) - half_len
    held = lambda a: np.ascontiguousarray(a).astype(ml_dtypes.bfloat16)
    return dict(
        sub=sub,
        lane=lane,
        scale=1.0 / (count * count),
        to_col=held(waves(pixels, lane)),
        to_row=held(waves(pixels, sub).T),
        from_col=held(waves(pixels, lane).T),
        from_row=held(waves(pixels, sub)),
        tap_col=held(waves(taps, lane)),
        tap_row=held(waves(taps, sub).T),
    )


def dot(a, b, contract=((1,), (0,))):
    return lax.dot_general(a, b, (contract, ((), ())), preferred_element_type=F32)


def weigh(waves, tables):
    sub, lane = tables.shape[0] // 2, tables.shape[1] // 2
    (cc, cs), (sc, ss) = [(a[:, :lane], a[:, lane:]) for a in waves]
    pa, pb, qa, qb = tables[:sub, :lane], tables[:sub, lane:], tables[sub:, :lane], tables[sub:, lane:]
    return (
        (pa * cc + pb * cs + qa * sc + qb * ss).astype(BF16),
        (pa * cs - pb * cc + qa * ss - qb * sc).astype(BF16),
        (pa * sc + pb * ss - qa * cc - qb * cs).astype(BF16),
        (pa * ss - pb * sc - qa * cs + qb * cc).astype(BF16),
    )


def convolve_kernel(plan, *refs):
    n_in, n_out = plan["n_in"], plan["n_out"]
    sources, outs, held = refs[:n_in], refs[n_in : n_in + n_out], refs[n_in + n_out :]
    local, (sems, out_sems, row_waves, col_waves, back, heads, done, head_rows) = held[:n_in], held[n_in:]
    sub, lane, rows, nb, cap, slots = (plan[k] for k in ("sub", "lane", "rows", "nb", "cap", "slots"))
    copies = [pltpu.make_async_copy(a, b, sems.at[i]) for i, (a, b) in enumerate(zip(sources[:-1], local[:-1]))]
    tiles = [
        pltpu.make_async_copy(sources[-1].at[s], local[-1].at[s], sems.at[n_in - 1 + s]) for s in range(slots)
    ]
    for copy in copies + tiles:
        copy.start()
    owner, local_id, valid, visit, inv_var, coef, kx, ky, to_col, to_row, from_col, from_row, tap_col, tap_row, patch = local
    for copy in copies:
        copy.wait()
    side = patch.shape[1]
    row_waves[...] = dot(tap_row[...], ky[...], ((1,), (1,)))
    col_waves[...] = (dot(kx[...], tap_col[...]) * plan["scale"]).astype(BF16)
    band = lax.axis_index("band")
    for phase in range(nb):
        start = pl.multiple_of(plan["chunk"](band, phase) * rows, rows)
        back[phase * rows : (phase + 1) * rows, :] = from_row[pl.ds(start, rows), :]
    heads[...] = jnp.full(heads.shape, -1.0, F32)
    me = lax.axis_index("sky")
    basis = kx.shape[0]
    lanes = lax.broadcasted_iota(jnp.int32, (1, 128), 1)

    row_ids = lax.broadcasted_iota(jnp.int32, (side, side), 0)

    def mixing(slot):
        seen = visit[0, slot]
        weight = jnp.full((1, basis), inv_var[0, seen], F32).astype(BF16).astype(F32)
        return (weight * coef[seen].astype(BF16).astype(F32)).astype(BF16).astype(F32)

    def sent(slot, phase, ref):
        return pltpu.make_async_copy(done.at[slot, phase * rows : (phase + 1) * rows, :], ref, out_sems.at[slot, phase])

    def deliver(slot, full):
        done[slot] = full
        mine = owner[0, slot]
        rank = jnp.int32(0)
        for other in range(slots):
            rank = rank + jnp.where((other < slot) & (owner[0, other] == mine), 1, 0).astype(jnp.int32)
        box = mine if plan["single"] else mine ^ me
        weight = jnp.full((1, 128), inv_var[0, visit[0, slot]], F32)
        facts = jnp.where(lanes == 8 * rank, local_id[0, slot].astype(F32), heads[box])
        facts = jnp.where(lanes == 8 * rank + 1, valid[0, slot].astype(F32), facts)
        heads[box] = jnp.where(lanes == 8 * rank + 2, weight, facts)
        def store(box):
            for phase in range(nb):
                ref, at, first = plan["place"](outs, box, phase)
                start = pl.multiple_of(first + rank * rows, rows)
                sent(slot, phase, ref.at[at, pl.ds(start, rows), :]).start()

        if plan["single"]:
            store(mine)
        else:
            for index in range(plan["sky"]):
                pl.when(box == index)(functools.partial(store, index))

    for batch in range(0, slots, BATCH):
        group = range(batch, min(batch + BATCH, slots))
        for s in group:
            tiles[s].wait()
        masked = [jnp.where(row_ids < valid[0, s], patch[s], 0.0).astype(BF16) for s in group]
        mixed = [(row_waves[...] * mixing(s)).astype(BF16) for s in group]
        col = dot(jnp.concatenate(masked, axis=0), to_col[...]).astype(BF16)
        tables = dot(jnp.concatenate(mixed, axis=0), col_waves[...])
        cos, sin = [], []
        for n, s in enumerate(group):
            mine = col[n * side : (n + 1) * side]
            both = dot(to_row[...], mine)
            y_cc, y_cs, y_sc, y_ss = weigh((both[:sub], both[sub:]), tables[n * 2 * sub : (n + 1) * 2 * sub])
            cos, sin = cos + [y_cc, y_sc], sin + [y_cs, y_ss]
        half = dot(jnp.concatenate(cos, axis=0), from_col[:lane, :])
        half = half + dot(jnp.concatenate(sin, axis=0), from_col[lane:, :])
        half = half.astype(BF16)
        for n, s in enumerate(group):
            full = dot(back[...], half[n * 2 * sub : (n + 1) * 2 * sub])
            deliver(s, full.astype(BF16))
    width = patch.shape[2]
    copies = []
    for index in range(plan["sky"]):
        ref, at, first = plan["head"](outs, index)
        row = jnp.concatenate([heads[index]] * (width // 128), axis=1)
        head_rows[index] = jnp.broadcast_to(row, (HEAD, width)).astype(BF16)
        copies.append(pltpu.make_async_copy(head_rows.at[index], ref.at[at, first : first + HEAD, :], sems.at[index]))
        copies[-1].start()
    for copy in copies:
        copy.wait()
    for slot in range(slots):
        for phase in range(nb):
            sent(slot, phase, plan["place"](outs, 0, phase)[0].at[0, 0:rows, :]).wait()


def sum_kernel(plan, phase, *refs):
    sky, nb, rows, cap, per = plan["sky"], plan["nb"], plan["rows"], plan["cap"], plan["per"]
    first, last = phase == 0, phase == nb - 1
    refs = list(refs)
    take = lambda n: [refs.pop(0) for _ in range(n)]
    boxes = take(plan["n_boxes"])
    arrived = take(len(plan["adds"][phase]))
    heads = take(plan["n_boxes"]) if first else None
    facts = None if first else take(2)
    if not first:
        take(1)
    band_out, extra = take(2)
    if first:
        facts = take(2)
    acc, cov, sems = take(3)
    if first:
        whole_facts, weights = take(2)
        rows_of = [h[d, 0:1, :128].astype(F32) for h in heads for d in range(h.shape[0])]
        for source, row in enumerate(rows_of):
            whole_facts[source : source + 1, :] = row.astype(jnp.int32)
            weights[source : source + 1, :] = row
        copies = [pltpu.make_async_copy(a, b, sems.at[i]) for i, (a, b) in enumerate(((whole_facts, facts[0]), (weights, facts[1])))]
        for copy in copies:
            copy.start()
    chunk = plan["chunk"](lax.axis_index("band"), phase)
    acc[...] = jnp.zeros_like(acc)
    cov[...] = jnp.zeros_like(cov)
    row_ids = chunk * rows + lax.broadcasted_iota(jnp.int32, (rows, 128), 0)
    if first:
        for copy in copies:
            copy.wait()
    for source in range(sky):
        group, at = (0, source) if plan["single"] else (source, 0)
        for rank in range(cap):
            local = facts[0][source, 8 * rank]

            @pl.when(local >= 0)
            def _(group=group, at=at, rank=rank, source=source, local=local):
                acc[local] += boxes[group][at, rank * rows : (rank + 1) * rows, :].astype(F32)
                weight = jnp.full((rows, 128), facts[1][source, 8 * rank + 2], F32)
                cov[local] += jnp.where(row_ids < facts[0][source, 8 * rank + 1], weight, 0.0)

    width = acc.shape[2]
    copies = []
    for patch in range(per):
        factor = 1.0 / jnp.maximum(cov[patch], 1.0)
        for at in range(0, width, 128):
            value = acc[patch, :, at : at + 128] * factor
            acc[patch, :, at : at + 128] = value
            for other in arrived:
                value = value + other[patch, :, at : at + 128].astype(F32)
            extra[patch, :, at : at + 128] = value.astype(extra.dtype)
        copies.append(pltpu.make_async_copy(
            acc.at[patch], band_out.at[patch, pl.ds(pl.multiple_of(chunk * rows, rows), rows), :], sems.at[patch]))
        copies[-1].start()
    for copy in copies:
        copy.wait()


def band_plan(nb):
    shifts = list(range(1, nb)) + [0]
    return lambda band, phase: (
        (band + shifts[phase]) % nb if isinstance(band, int) else lax.rem(band + shifts[phase], nb)
    )


def copy_kernel(source, out):
    out[...] = source[...]


def brought(array):
    return pl.pallas_call(
        copy_kernel, out_shape=jax.ShapeDtypeStruct(array.shape, array.dtype),
        compiler_params=pltpu.CompilerParams(vmem_limit_bytes=SUM_VMEM * MIB), name="bring",
    )(array)


def accumulate_kernel(*refs):
    total, *terms, out = refs
    value = total[...]
    for term in terms:
        value = value + term[...].astype(F32)
    out[...] = value


def per_device(patches, valid_rows, slot_owner, slot_local, slot_visit, basis_coef, inv_var, kernel_x, kernel_y):
    tiles = patches[0]
    slots, side, width = tiles.shape
    sky, nb = lax.axis_size("sky"), lax.axis_size("band")
    cap = max(2, 2 * slots // sky)
    rows = side // nb
    single = sky != 4
    tables = wave_tables(side, kernel_x.shape[1])
    sub, lane = tables["sub"], tables["lane"]
    chunk = band_plan(nb)
    late = min(3, nb - 1)
    adds = [[]] * (nb - 1) + [list(range(nb - 1 - late))]
    box = cap * rows
    shaped = lambda count, height: jax.ShapeDtypeStruct((count, height, width), BF16)
    if single:
        out_shapes = [shaped(sky, box + (HEAD if phase == 0 else 0)) for phase in range(nb)]
        place = lambda outs, dest, phase: (outs[phase], dest, 0)
        head = lambda outs, dest: (outs[0], dest, box)
    else:
        far = lambda phase: shaped(1, box + (HEAD if phase == 0 else 0))
        out_shapes = [shaped(1, nb * box + HEAD)] * 2 + [far(phase) for phase in range(nb) for _ in range(2)]

        def place(outs, dest, phase):
            return (outs[dest], 0, phase * box) if dest < 2 else (outs[2 * phase + dest], 0, 0)

        def head(outs, dest):
            return outs[dest], 0, nb * box if dest < 2 else box

    plan = dict(sub=sub, lane=lane, rows=rows, nb=nb, scale=tables["scale"], slots=slots, cap=cap, sky=sky, per=PATCH_DEV,
                single=single, n_boxes=1 if single else sky, place=place, head=head, chunk=chunk, adds=adds)
    smem = pl.BlockSpec(memory_space=pltpu.SMEM)
    hbm = pl.BlockSpec(memory_space=pltpu.HBM)
    consts = [jnp.asarray(tables[n]) for n in ("to_col", "to_row", "from_col", "from_row", "tap_col", "tap_row")]
    args = [slot_owner.reshape(1, slots), slot_local, valid_rows, slot_visit, inv_var, basis_coef.transpose(1, 0, 2),
            kernel_x, kernel_y] + consts + [tiles]
    plan.update(n_in=len(args), n_out=len(out_shapes))
    landing = [pltpu.SMEM(a.shape, a.dtype) for a in args[:5]] + [pltpu.VMEM(a.shape, a.dtype) for a in args[5:]]
    sent = pl.pallas_call(
        functools.partial(convolve_kernel, plan),
        out_shape=out_shapes,
        in_specs=[hbm] * len(args),
        out_specs=[hbm] * len(out_shapes),
        scratch_shapes=landing + [
            pltpu.SemaphoreType.DMA((max(len(args) - 1 + slots, sky),)), pltpu.SemaphoreType.DMA((slots, nb)),
            pltpu.VMEM((2 * sub, kernel_x.shape[0]), F32),
            pltpu.VMEM((kernel_x.shape[0], 2 * lane), BF16), pltpu.VMEM((side, 2 * sub), BF16),
            pltpu.VMEM((sky, 1, 128), F32),
            pltpu.VMEM((slots, side, width), BF16), pltpu.VMEM((sky, HEAD, width), BF16)],
        compiler_params=pltpu.CompilerParams(vmem_limit_bytes=CONV_VMEM * MIB),
        cost_estimate=pl.CostEstimate(flops=slots * 22 * side**3, bytes_accessed=slots * side * side * 6,
                                      transcendentals=0),
        name="convolve",
    )(*args)

    swap = lambda a, r: a if r == 0 else lax.ppermute(a, "sky", [(i, i ^ r) for i in range(sky)])
    if single:
        moved = [lax.all_to_all(s, "sky", split_axis=0, concat_axis=0, tiled=True) for s in sent]
        pieces = lambda phase: [(moved[phase], sky, 0, 0, box)]
    else:
        own, near, far = sent[0], swap(sent[1], 1), []
        for i, array in enumerate(sent[2:]):
            if i == 2 and STAGE:
                own, array = lax.optimization_barrier((brought(own), array))
            far.append(swap(array, 2 + i % 2))

        def pieces(phase):
            here = [(a, 1, 0, phase, nb * box) for a in (own, near)]
            return here + [(a, 1, 0, 0, box) for a in far[2 * phase : 2 * phase + 2]]

    band_buf, facts, arrived = None, None, []
    band_shape = jax.ShapeDtypeStruct((PATCH_DEV, side, width), F32)
    chunk_shape = (PATCH_DEV, rows, width)
    whole = lambda shape: pl.BlockSpec(shape, lambda *_: (0,) * len(shape))
    fact_shapes = [jax.ShapeDtypeStruct((sky, 128), jnp.int32), jax.ShapeDtypeStruct((sky, 128), F32)]
    for phase in range(nb):
        first, last = phase == 0, phase == nb - 1
        inputs, specs = [], []
        for array, count, at, row, _ in pieces(phase):
            inputs.append(array)
            specs.append(pl.BlockSpec((count, box, width), lambda i, at=at, row=row: (at, row, 0)))
        for earlier in adds[phase]:
            inputs.append(arrived[earlier])
            specs.append(whole(chunk_shape))
        outs = [band_shape, jax.ShapeDtypeStruct(chunk_shape, F32 if last else BF16)]
        out_specs, aliases, scratch = [hbm, whole(chunk_shape)], {}, []
        if first:
            for array, count, at, _, end in pieces(phase):
                inputs.append(array)
                specs.append(pl.BlockSpec((count, HEAD, width), lambda i, at=at, end=end: (at, end // HEAD, 0)))
            outs, out_specs = outs + fact_shapes, out_specs + [smem] * 2
            scratch = [pltpu.VMEM(s.shape, s.dtype) for s in fact_shapes]
        else:
            inputs, specs = inputs + facts, specs + [smem] * 2
            aliases = {len(inputs): 0}
            inputs, specs = inputs + [band_buf], specs + [hbm]
        band_buf, extra, *rest = pl.pallas_call(
            functools.partial(sum_kernel, plan, phase),
            grid=(1,),
            out_shape=outs,
            in_specs=specs,
            out_specs=out_specs,
            scratch_shapes=[pltpu.VMEM(chunk_shape, F32), pltpu.VMEM((PATCH_DEV, rows, 128), F32),
                            pltpu.SemaphoreType.DMA((PATCH_DEV,))] + scratch,
            input_output_aliases=aliases,
            compiler_params=pltpu.CompilerParams(vmem_limit_bytes=SUM_VMEM * MIB),
            cost_estimate=pl.CostEstimate(flops=4 * PATCH_DEV * rows * width,
                                          bytes_accessed=12 * PATCH_DEV * rows * width, transcendentals=0),
            name="add_up",
        )(*inputs)
        facts = rest if first else facts
        if not last:
            arrived.append(lax.ppermute(extra, "band", [(b, chunk(b, phase)) for b in range(nb)]))
    if late:
        terms = arrived[nb - 1 - late :]
        for i in range(late - 1):
            extra, terms[i] = lax.optimization_barrier((extra, terms[i]))
        extra = pl.pallas_call(
            accumulate_kernel, grid=(1,), out_shape=jax.ShapeDtypeStruct(chunk_shape, F32),
            in_specs=[whole(chunk_shape)] * (1 + late), out_specs=whole(chunk_shape), input_output_aliases={0: 0},
            compiler_params=pltpu.CompilerParams(vmem_limit_bytes=SUM_VMEM * MIB), name="accumulate",
        )(extra, *terms)
    return (band_buf[None], extra)


def solution(mesh):
    in_specs = (
        P(("tract", "band"), "sky", None, None),
        P(("tract", "band"), "sky"),
        P(("tract", "band"), "sky", None),
        P(("tract", "band"), "sky"),
        P(("tract", "band"), "sky"),
        P(("tract", "band"), None, None),
        P(("tract", "band"), None),
        P(),
        P(),
    )
    out_specs = (P(("tract", "band"), "sky", None, None), P(("tract", "sky"), "band", None))
    return jax.shard_map(per_device, mesh=mesh, in_specs=in_specs, out_specs=out_specs, check_vma=False)
```

```python
import functools

import jax
import jax.numpy as jnp
import ml_dtypes
import numpy as np
from jax import lax
from jax.experimental import pallas as pl
from jax.experimental.pallas import tpu as pltpu
from jax.sharding import PartitionSpec as P

PATCH_DEV = 8
F32, BF16 = jnp.float32, jnp.bfloat16
MIB = 1024 * 1024
HEAD = 16
BATCH = 4
CONV_VMEM = 64
SUM_VMEM = 24


def round_up(value, multiple):
    return -(-value // multiple) * multiple


def wave_tables(side, kernel_len):
    half_len = kernel_len // 2
    count = -(-(side + half_len) // 2)
    omega = np.pi * (np.arange(count) + 0.5) / count
    sub, lane = round_up(count, 16), round_up(count, 128)

    def waves(points, width):
        out = np.zeros((len(points), 2 * width), np.float64)
        out[:, :count] = np.cos(np.outer(points, omega))
        out[:, width : width + count] = np.sin(np.outer(points, omega))
        return out

    pixels, taps = np.arange(side), np.arange(kernel_len) - half_len
    held = lambda a: np.ascontiguousarray(a).astype(ml_dtypes.bfloat16)
    return dict(
        sub=sub,
        lane=lane,
        scale=1.0 / (count * count),
        to_col=held(waves(pixels, lane)),
        to_row=held(waves(pixels, sub).T),
        from_col=held(waves(pixels, lane).T),
        from_row=held(waves(pixels, sub)),
        tap_col=held(waves(taps, lane)),
        tap_row=held(waves(taps, sub).T),
    )


def dot(a, b, contract=((1,), (0,))):
    return lax.dot_general(a, b, (contract, ((), ())), preferred_element_type=F32)


def weigh(waves, tables):
    sub, lane = tables.shape[0] // 2, tables.shape[1] // 2
    (cc, cs), (sc, ss) = [(a[:, :lane], a[:, lane:]) for a in waves]
    pa, pb, qa, qb = tables[:sub, :lane], tables[:sub, lane:], tables[sub:, :lane], tables[sub:, lane:]
    return (
        (pa * cc + pb * cs + qa * sc + qb * ss).astype(BF16),
        (pa * cs - pb * cc + qa * ss - qb * sc).astype(BF16),
        (pa * sc + pb * ss - qa * cc - qb * cs).astype(BF16),
        (pa * ss - pb * sc - qa * cs + qb * cc).astype(BF16),
    )


def convolve_kernel(plan, *refs):
    n_in, n_out = plan["n_in"], plan["n_out"]
    sources, outs, held = refs[:n_in], refs[n_in : n_in + n_out], refs[n_in + n_out :]
    local, (sems, out_sems, row_waves, col_waves, back, heads, done, head_rows) = held[:n_in], held[n_in:]
    sub, lane, rows, nb, cap, slots = (plan[k] for k in ("sub", "lane", "rows", "nb", "cap", "slots"))
    copies = [pltpu.make_async_copy(a, b, sems.at[i]) for i, (a, b) in enumerate(zip(sources[:-1], local[:-1]))]
    tiles = [
        pltpu.make_async_copy(sources[-1].at[s], local[-1].at[s], sems.at[n_in - 1 + s]) for s in range(slots)
    ]
    for copy in copies + tiles:
        copy.start()
    owner, local_id, valid, visit, inv_var, coef, kx, ky, to_col, to_row, from_col, from_row, tap_col, tap_row, patch = local
    for copy in copies:
        copy.wait()
    side = patch.shape[1]
    row_waves[...] = dot(tap_row[...], ky[...], ((1,), (1,)))
    col_waves[...] = (dot(kx[...], tap_col[...]) * plan["scale"]).astype(BF16)
    band = lax.axis_index("band")
    for phase in range(nb):
        start = pl.multiple_of(plan["chunk"](band, phase) * rows, rows)
        back[phase * rows : (phase + 1) * rows, :] = from_row[pl.ds(start, rows), :]
    heads[...] = jnp.full(heads.shape, -1.0, F32)
    me = lax.axis_index("sky")
    basis = kx.shape[0]
    lanes = lax.broadcasted_iota(jnp.int32, (1, 128), 1)

    row_ids = lax.broadcasted_iota(jnp.int32, (side, side), 0)

    def mixing(slot):
        seen = visit[0, slot]
        weight = jnp.full((1, basis), inv_var[0, seen], F32).astype(BF16).astype(F32)
        return (weight * coef[seen].astype(BF16).astype(F32)).astype(BF16).astype(F32)

    def sent(slot, phase, ref):
        return pltpu.make_async_copy(done.at[slot, phase * rows : (phase + 1) * rows, :], ref, out_sems.at[slot, phase])

    def deliver(slot, full):
        done[slot] = full
        mine = owner[0, slot]
        rank = jnp.int32(0)
        for other in range(slots):
            rank = rank + jnp.where((other < slot) & (owner[0, other] == mine), 1, 0).astype(jnp.int32)
        box = mine if plan["single"] else mine ^ me
        weight = jnp.full((1, 128), inv_var[0, visit[0, slot]], F32)
        facts = jnp.where(lanes == 8 * rank, local_id[0, slot].astype(F32), heads[box])
        facts = jnp.where(lanes == 8 * rank + 1, valid[0, slot].astype(F32), facts)
        heads[box] = jnp.where(lanes == 8 * rank + 2, weight, facts)
        def store(box):
            for phase in range(nb):
                ref, at, first = plan["place"](outs, box, phase)
                start = pl.multiple_of(first + rank * rows, rows)
                sent(slot, phase, ref.at[at, pl.ds(start, rows), :]).start()

        if plan["single"]:
            store(mine)
        else:
            for index in range(plan["sky"]):
                pl.when(box == index)(functools.partial(store, index))

    for batch in range(0, slots, BATCH):
        group = range(batch, min(batch + BATCH, slots))
        for s in group:
            tiles[s].wait()
        masked = [jnp.where(row_ids < valid[0, s], patch[s], 0.0).astype(BF16) for s in group]
        mixed = [(row_waves[...] * mixing(s)).astype(BF16) for s in group]
        col = dot(jnp.concatenate(masked, axis=0), to_col[...]).astype(BF16)
        tables = dot(jnp.concatenate(mixed, axis=0), col_waves[...])
        cos, sin = [], []
        for n, s in enumerate(group):
            mine = col[n * side : (n + 1) * side]
            both = dot(to_row[...], mine)
            y_cc, y_cs, y_sc, y_ss = weigh((both[:sub], both[sub:]), tables[n * 2 * sub : (n + 1) * 2 * sub])
            cos, sin = cos + [y_cc, y_sc], sin + [y_cs, y_ss]
        half = dot(jnp.concatenate(cos, axis=0), from_col[:lane, :])
        half = half + dot(jnp.concatenate(sin, axis=0), from_col[lane:, :])
        half = half.astype(BF16)
        for n, s in enumerate(group):
            full = dot(back[...], half[n * 2 * sub : (n + 1) * 2 * sub])
            deliver(s, full.astype(BF16))
    width = patch.shape[2]
    copies = []
    for index in range(plan["sky"]):
        ref, at, first = plan["head"](outs, index)
        row = jnp.concatenate([heads[index]] * (width // 128), axis=1)
        head_rows[index] = jnp.broadcast_to(row, (HEAD, width)).astype(BF16)
        copies.append(pltpu.make_async_copy(head_rows.at[index], ref.at[at, first : first + HEAD, :], sems.at[index]))
        copies[-1].start()
    for copy in copies:
        copy.wait()
    for slot in range(slots):
        for phase in range(nb):
            sent(slot, phase, plan["place"](outs, 0, phase)[0].at[0, 0:rows, :]).wait()


def sum_kernel(plan, phase, *refs):
    sky, nb, rows, cap, per = plan["sky"], plan["nb"], plan["rows"], plan["cap"], plan["per"]
    first, last = phase == 0, phase == nb - 1
    refs = list(refs)
    take = lambda n: [refs.pop(0) for _ in range(n)]
    boxes = take(plan["n_boxes"])
    arrived = take(len(plan["adds"][phase]))
    heads = take(plan["n_boxes"]) if first else None
    facts = None if first else take(2)
    if not first:
        take(1)
    band_out, extra = take(2)
    if first:
        facts = take(2)
    acc, cov, sems = take(3)
    if first:
        whole_facts, weights = take(2)
        rows_of = [h[d, 0:1, :128].astype(F32) for h in heads for d in range(h.shape[0])]
        for source, row in enumerate(rows_of):
            whole_facts[source : source + 1, :] = row.astype(jnp.int32)
            weights[source : source + 1, :] = row
        copies = [pltpu.make_async_copy(a, b, sems.at[i]) for i, (a, b) in enumerate(((whole_facts, facts[0]), (weights, facts[1])))]
        for copy in copies:
            copy.start()
    chunk = plan["chunk"](lax.axis_index("band"), phase)
    acc[...] = jnp.zeros_like(acc)
    cov[...] = jnp.zeros_like(cov)
    row_ids = chunk * rows + lax.broadcasted_iota(jnp.int32, (rows, 128), 0)
    if first:
        for copy in copies:
            copy.wait()
    for source in range(sky):
        group, at = (0, source) if plan["single"] else (source, 0)
        for rank in range(cap):
            local = facts[0][source, 8 * rank]

            @pl.when(local >= 0)
            def _(group=group, at=at, rank=rank, source=source, local=local):
                acc[local] += boxes[group][at, rank * rows : (rank + 1) * rows, :].astype(F32)
                weight = jnp.full((rows, 128), facts[1][source, 8 * rank + 2], F32)
                cov[local] += jnp.where(row_ids < facts[0][source, 8 * rank + 1], weight, 0.0)

    width = acc.shape[2]
    copies = []
    for patch in range(per):
        factor = 1.0 / jnp.maximum(cov[patch], 1.0)
        for at in range(0, width, 128):
            value = acc[patch, :, at : at + 128] * factor
            acc[patch, :, at : at + 128] = value
            for other in arrived:
                value = value + other[patch, :, at : at + 128].astype(F32)
            extra[patch, :, at : at + 128] = value.astype(extra.dtype)
        copies.append(pltpu.make_async_copy(
            acc.at[patch], band_out.at[patch, pl.ds(pl.multiple_of(chunk * rows, rows), rows), :], sems.at[patch]))
        copies[-1].start()
    for copy in copies:
        copy.wait()


def band_plan(nb):
    shifts = list(range(1, nb)) + [0]
    return lambda band, phase: (
        (band + shifts[phase]) % nb if isinstance(band, int) else lax.rem(band + shifts[phase], nb)
    )


def copy_kernel(source, out):
    out[...] = source[...]


def brought(array):
    return pl.pallas_call(
        copy_kernel, out_shape=jax.ShapeDtypeStruct(array.shape, array.dtype),
        compiler_params=pltpu.CompilerParams(vmem_limit_bytes=SUM_VMEM * MIB), name="bring",
    )(array)


def accumulate_kernel(*refs):
    total, *terms, out, held, sems = refs
    copies = []
    for patch in range(total.shape[0]):
        value = total[patch]
        for term in terms:
            value = value + term[patch].astype(F32)
        held[patch] = value
        copies.append(pltpu.make_async_copy(held.at[patch], out.at[patch], sems.at[patch]))
        copies[-1].start()
    for copy in copies:
        copy.wait()


def per_device(patches, valid_rows, slot_owner, slot_local, slot_visit, basis_coef, inv_var, kernel_x, kernel_y):
    tiles = patches[0]
    slots, side, width = tiles.shape
    sky, nb = lax.axis_size("sky"), lax.axis_size("band")
    cap = max(2, 2 * slots // sky)
    rows = side // nb
    single = sky != 4
    tables = wave_tables(side, kernel_x.shape[1])
    sub, lane = tables["sub"], tables["lane"]
    chunk = band_plan(nb)
    late = min(3, nb - 1)
    adds = [[]] * (nb - 1) + [list(range(nb - 1 - late))]
    box = cap * rows
    shaped = lambda count, height: jax.ShapeDtypeStruct((count, height, width), BF16)
    if single:
        out_shapes = [shaped(sky, box + (HEAD if phase == 0 else 0)) for phase in range(nb)]
        place = lambda outs, dest, phase: (outs[phase], dest, 0)
        head = lambda outs, dest: (outs[0], dest, box)
    else:
        far = lambda phase: shaped(1, box + (HEAD if phase == 0 else 0))
        out_shapes = [shaped(1, nb * box + HEAD)] * 2 + [far(phase) for phase in range(nb) for _ in range(2)]

        def place(outs, dest, phase):
            return (outs[dest], 0, phase * box) if dest < 2 else (outs[2 * phase + dest], 0, 0)

        def head(outs, dest):
            return outs[dest], 0, nb * box if dest < 2 else box

    plan = dict(sub=sub, lane=lane, rows=rows, nb=nb, scale=tables["scale"], slots=slots, cap=cap, sky=sky, per=PATCH_DEV,
                single=single, n_boxes=1 if single else sky, place=place, head=head, chunk=chunk, adds=adds)
    smem = pl.BlockSpec(memory_space=pltpu.SMEM)
    hbm = pl.BlockSpec(memory_space=pltpu.HBM)
    consts = [jnp.asarray(tables[n]) for n in ("to_col", "to_row", "from_col", "from_row", "tap_col", "tap_row")]
    args = [slot_owner.reshape(1, slots), slot_local, valid_rows, slot_visit, inv_var, basis_coef.transpose(1, 0, 2),
            kernel_x, kernel_y] + consts + [tiles]
    plan.update(n_in=len(args), n_out=len(out_shapes))
    landing = [pltpu.SMEM(a.shape, a.dtype) for a in args[:5]] + [pltpu.VMEM(a.shape, a.dtype) for a in args[5:]]
    sent = pl.pallas_call(
        functools.partial(convolve_kernel, plan),
        out_shape=out_shapes,
        in_specs=[hbm] * len(args),
        out_specs=[hbm] * len(out_shapes),
        scratch_shapes=landing + [
            pltpu.SemaphoreType.DMA((max(len(args) - 1 + slots, sky),)), pltpu.SemaphoreType.DMA((slots, nb)),
            pltpu.VMEM((2 * sub, kernel_x.shape[0]), F32),
            pltpu.VMEM((kernel_x.shape[0], 2 * lane), BF16), pltpu.VMEM((side, 2 * sub), BF16),
            pltpu.VMEM((sky, 1, 128), F32),
            pltpu.VMEM((slots, side, width), BF16), pltpu.VMEM((sky, HEAD, width), BF16)],
        compiler_params=pltpu.CompilerParams(vmem_limit_bytes=CONV_VMEM * MIB),
        cost_estimate=pl.CostEstimate(flops=slots * 22 * side**3, bytes_accessed=slots * side * side * 6,
                                      transcendentals=0),
        name="convolve",
    )(*args)

    swap = lambda a, r: a if r == 0 else lax.ppermute(a, "sky", [(i, i ^ r) for i in range(sky)])
    if single:
        moved = [lax.all_to_all(s, "sky", split_axis=0, concat_axis=0, tiled=True) for s in sent]
        pieces = lambda phase: [(moved[phase], sky, 0, 0, box)]
    else:
        own, second = lax.optimization_barrier((brought(sent[0]), sent[4]))
        near = swap(sent[1], 1)
        far = [swap(a, 2 + i % 2) for i, a in enumerate([*sent[2:4], second, *sent[5:]])]

        def pieces(phase):
            here = [(a, 1, 0, phase, nb * box) for a in (own, near)]
            return here + [(a, 1, 0, 0, box) for a in far[2 * phase : 2 * phase + 2]]

    band_buf, facts, arrived = None, None, []
    band_shape = jax.ShapeDtypeStruct((PATCH_DEV, side, width), F32)
    chunk_shape = (PATCH_DEV, rows, width)
    whole = lambda shape: pl.BlockSpec(shape, lambda *_: (0,) * len(shape))
    fact_shapes = [jax.ShapeDtypeStruct((sky, 128), jnp.int32), jax.ShapeDtypeStruct((sky, 128), F32)]
    for phase in range(nb):
        first, last = phase == 0, phase == nb - 1
        inputs, specs = [], []
        for array, count, at, row, _ in pieces(phase):
            inputs.append(array)
            specs.append(pl.BlockSpec((count, box, width), lambda i, at=at, row=row: (at, row, 0)))
        for earlier in adds[phase]:
            inputs.append(arrived[earlier])
            specs.append(whole(chunk_shape))
        outs = [band_shape, jax.ShapeDtypeStruct(chunk_shape, F32 if last else BF16)]
        out_specs, aliases, scratch = [hbm, whole(chunk_shape)], {}, []
        if first:
            for array, count, at, _, end in pieces(phase):
                inputs.append(array)
                specs.append(pl.BlockSpec((count, HEAD, width), lambda i, at=at, end=end: (at, end // HEAD, 0)))
            outs, out_specs = outs + fact_shapes, out_specs + [smem] * 2
            scratch = [pltpu.VMEM(s.shape, s.dtype) for s in fact_shapes]
        else:
            inputs, specs = inputs + facts, specs + [smem] * 2
            aliases = {len(inputs): 0}
            inputs, specs = inputs + [band_buf], specs + [hbm]
        band_buf, extra, *rest = pl.pallas_call(
            functools.partial(sum_kernel, plan, phase),
            grid=(1,),
            out_shape=outs,
            in_specs=specs,
            out_specs=out_specs,
            scratch_shapes=[pltpu.VMEM(chunk_shape, F32), pltpu.VMEM((PATCH_DEV, rows, 128), F32),
                            pltpu.SemaphoreType.DMA((PATCH_DEV,))] + scratch,
            input_output_aliases=aliases,
            compiler_params=pltpu.CompilerParams(vmem_limit_bytes=SUM_VMEM * MIB),
            cost_estimate=pl.CostEstimate(flops=4 * PATCH_DEV * rows * width,
                                          bytes_accessed=12 * PATCH_DEV * rows * width, transcendentals=0),
            name="add_up",
        )(*inputs)
        facts = rest if first else facts
        if not last:
            arrived.append(lax.ppermute(extra, "band", [(b, chunk(b, phase)) for b in range(nb)]))
    if late:
        terms = arrived[nb - 1 - late :]
        for i in range(late - 1):
            extra, terms[i] = lax.optimization_barrier((extra, terms[i]))
        extra = pl.pallas_call(
            accumulate_kernel, grid=(1,), out_shape=jax.ShapeDtypeStruct(chunk_shape, F32),
            in_specs=[whole(chunk_shape)] * (1 + late), out_specs=hbm,
            scratch_shapes=[pltpu.VMEM(chunk_shape, F32), pltpu.SemaphoreType.DMA((PATCH_DEV,))],
            compiler_params=pltpu.CompilerParams(vmem_limit_bytes=SUM_VMEM * MIB), name="accumulate",
        )(extra, *terms)
    return (band_buf[None], extra)


def solution(mesh):
    in_specs = (
        P(("tract", "band"), "sky", None, None),
        P(("tract", "band"), "sky"),
        P(("tract", "band"), "sky", None),
        P(("tract", "band"), "sky"),
        P(("tract", "band"), "sky"),
        P(("tract", "band"), None, None),
        P(("tract", "band"), None),
        P(),
        P(),
    )
    out_specs = (P(("tract", "band"), "sky", None, None), P(("tract", "sky"), "band", None))
    return jax.shard_map(per_device, mesh=mesh, in_specs=in_specs, out_specs=out_specs, check_vma=False)
```

```python
import functools

import jax
import jax.numpy as jnp
import ml_dtypes
import numpy as np
from jax import lax
from jax.experimental import pallas as pl
from jax.experimental.pallas import tpu as pltpu
from jax.sharding import PartitionSpec as P

PATCH_DEV = 8
F32, BF16 = jnp.float32, jnp.bfloat16
MIB = 1024 * 1024
HEAD = 16
BATCH = 4
CONV_VMEM = 64
SUM_VMEM = 24


def round_up(value, multiple):
    return -(-value // multiple) * multiple


def wave_tables(side, kernel_len):
    half_len = kernel_len // 2
    count = -(-(side + half_len) // 2)
    omega = np.pi * (np.arange(count) + 0.5) / count
    sub, lane = round_up(count, 16), round_up(count, 128)

    def waves(points, width):
        out = np.zeros((len(points), 2 * width), np.float64)
        out[:, :count] = np.cos(np.outer(points, omega))
        out[:, width : width + count] = np.sin(np.outer(points, omega))
        return out

    pixels, taps = np.arange(side), np.arange(kernel_len) - half_len
    held = lambda a: np.ascontiguousarray(a).astype(ml_dtypes.bfloat16)
    return dict(
        sub=sub,
        lane=lane,
        scale=1.0 / (count * count),
        to_col=held(waves(pixels, lane)),
        to_row=held(waves(pixels, sub).T),
        from_col=held(waves(pixels, lane).T),
        from_row=held(waves(pixels, sub)),
        tap_col=held(waves(taps, lane)),
        tap_row=held(waves(taps, sub).T),
    )


def dot(a, b, contract=((1,), (0,))):
    return lax.dot_general(a, b, (contract, ((), ())), preferred_element_type=F32)


def weigh(waves, tables):
    sub, lane = tables.shape[0] // 2, tables.shape[1] // 2
    (cc, cs), (sc, ss) = [(a[:, :lane], a[:, lane:]) for a in waves]
    pa, pb, qa, qb = tables[:sub, :lane], tables[:sub, lane:], tables[sub:, :lane], tables[sub:, lane:]
    return (
        (pa * cc + pb * cs + qa * sc + qb * ss).astype(BF16),
        (pa * cs - pb * cc + qa * ss - qb * sc).astype(BF16),
        (pa * sc + pb * ss - qa * cc - qb * cs).astype(BF16),
        (pa * ss - pb * sc - qa * cs + qb * cc).astype(BF16),
    )


def convolve_kernel(plan, *refs):
    n_in, n_out = plan["n_in"], plan["n_out"]
    sources, outs, held = refs[:n_in], refs[n_in : n_in + n_out], refs[n_in + n_out :]
    local, (sems, out_sems, row_waves, col_waves, back, heads, done, head_rows) = held[:n_in], held[n_in:]
    sub, lane, rows, nb, cap, slots = (plan[k] for k in ("sub", "lane", "rows", "nb", "cap", "slots"))
    copies = [pltpu.make_async_copy(a, b, sems.at[i]) for i, (a, b) in enumerate(zip(sources[:-1], local[:-1]))]
    tiles = [
        pltpu.make_async_copy(sources[-1].at[s], local[-1].at[s], sems.at[n_in - 1 + s]) for s in range(slots)
    ]
    for copy in copies + tiles:
        copy.start()
    owner, local_id, valid, visit, inv_var, coef, kx, ky, to_col, to_row, from_col, from_row, tap_col, tap_row, patch = local
    for copy in copies:
        copy.wait()
    side = patch.shape[1]
    row_waves[...] = dot(tap_row[...], ky[...], ((1,), (1,)))
    col_waves[...] = (dot(kx[...], tap_col[...]) * plan["scale"]).astype(BF16)
    band = lax.axis_index("band")
    for phase in range(nb):
        start = pl.multiple_of(plan["chunk"](band, phase) * rows, rows)
        back[phase * rows : (phase + 1) * rows, :] = from_row[pl.ds(start, rows), :]
    heads[...] = jnp.full(heads.shape, -1.0, F32)
    me = lax.axis_index("sky")
    basis = kx.shape[0]
    lanes = lax.broadcasted_iota(jnp.int32, (1, 128), 1)

    row_ids = lax.broadcasted_iota(jnp.int32, (side, side), 0)

    def mixing(slot):
        seen = visit[0, slot]
        weight = jnp.full((1, basis), inv_var[0, seen], F32).astype(BF16).astype(F32)
        return (weight * coef[seen].astype(BF16).astype(F32)).astype(BF16).astype(F32)

    def sent(slot, phase, ref):
        return pltpu.make_async_copy(done.at[slot, phase * rows : (phase + 1) * rows, :], ref, out_sems.at[slot, phase])

    def deliver(slot, full):
        done[slot] = full
        mine = owner[0, slot]
        rank = jnp.int32(0)
        for other in range(slots):
            rank = rank + jnp.where((other < slot) & (owner[0, other] == mine), 1, 0).astype(jnp.int32)
        box = mine if plan["single"] else mine ^ me
        weight = jnp.full((1, 128), inv_var[0, visit[0, slot]], F32)
        facts = jnp.where(lanes == 8 * rank, local_id[0, slot].astype(F32), heads[box])
        facts = jnp.where(lanes == 8 * rank + 1, valid[0, slot].astype(F32), facts)
        heads[box] = jnp.where(lanes == 8 * rank + 2, weight, facts)
        def store(box):
            for phase in range(nb):
                ref, at, first = plan["place"](outs, box, phase)
                start = pl.multiple_of(first + rank * rows, rows)
                sent(slot, phase, ref.at[at, pl.ds(start, rows), :]).start()

        if plan["single"]:
            store(mine)
        else:
            for index in range(plan["sky"]):
                pl.when(box == index)(functools.partial(store, index))

    for batch in range(0, slots, BATCH):
        group = range(batch, min(batch + BATCH, slots))
        for s in group:
            tiles[s].wait()
        masked = [jnp.where(row_ids < valid[0, s], patch[s], 0.0).astype(BF16) for s in group]
        mixed = [(row_waves[...] * mixing(s)).astype(BF16) for s in group]
        col = dot(jnp.concatenate(masked, axis=0), to_col[...]).astype(BF16)
        tables = dot(jnp.concatenate(mixed, axis=0), col_waves[...])
        cos, sin = [], []
        for n, s in enumerate(group):
            mine = col[n * side : (n + 1) * side]
            both = dot(to_row[...], mine)
            y_cc, y_cs, y_sc, y_ss = weigh((both[:sub], both[sub:]), tables[n * 2 * sub : (n + 1) * 2 * sub])
            cos, sin = cos + [y_cc, y_sc], sin + [y_cs, y_ss]
        half = dot(jnp.concatenate(cos, axis=0), from_col[:lane, :])
        half = half + dot(jnp.concatenate(sin, axis=0), from_col[lane:, :])
        half = half.astype(BF16)
        for n, s in enumerate(group):
            full = dot(back[...], half[n * 2 * sub : (n + 1) * 2 * sub])
            deliver(s, full.astype(BF16))
    width = patch.shape[2]
    copies = []
    for index in range(plan["sky"]):
        ref, at, first = plan["head"](outs, index)
        row = jnp.concatenate([heads[index]] * (width // 128), axis=1)
        head_rows[index] = jnp.broadcast_to(row, (HEAD, width)).astype(BF16)
        copies.append(pltpu.make_async_copy(head_rows.at[index], ref.at[at, first : first + HEAD, :], sems.at[index]))
        copies[-1].start()
    for copy in copies:
        copy.wait()
    for slot in range(slots):
        for phase in range(nb):
            sent(slot, phase, plan["place"](outs, 0, phase)[0].at[0, 0:rows, :]).wait()


def sum_kernel(plan, phase, *refs):
    sky, nb, rows, cap, per = plan["sky"], plan["nb"], plan["rows"], plan["cap"], plan["per"]
    first, last = phase == 0, phase == nb - 1
    refs = list(refs)
    take = lambda n: [refs.pop(0) for _ in range(n)]
    boxes = take(plan["n_boxes"])
    arrived = take(len(plan["adds"][phase]))
    facts = None if first else take(2)
    earlier = take(nb - 1) if last else []
    if last:
        band_out, extra = take(2)
    else:
        acc, extra = take(2)
    if first:
        facts = take(2)
    if last:
        acc, sems = take(2)
    (cov,) = take(1)
    if first:
        (fact_sems,) = take(1)
    if first:
        whole_facts, weights = take(2)
        rows_of = []
        for source in range(sky):
            group, at = (0, source) if plan["single"] else (source, 0)
            rows_of.append(boxes[group][at, plan["ends"][group] : plan["ends"][group] + HEAD, :128][0:1].astype(F32))
        for source, row in enumerate(rows_of):
            whole_facts[source : source + 1, :] = row.astype(jnp.int32)
            weights[source : source + 1, :] = row
        copies = [pltpu.make_async_copy(a, b, fact_sems.at[i]) for i, (a, b) in enumerate(((whole_facts, facts[0]), (weights, facts[1])))]
        for copy in copies:
            copy.start()
    band = lax.axis_index("band")
    chunk = plan["chunk"](band, phase)

    def out_rows(patch, at):
        return band_out.at[patch, pl.ds(pl.multiple_of(plan["chunk"](band, at) * rows, rows), rows), :]

    writes = []
    for at, done in enumerate(earlier):
        for patch in range(per):
            writes.append(pltpu.make_async_copy(done.at[patch], out_rows(patch, at), sems.at[at, patch]))
            writes[-1].start()
    acc[...] = jnp.zeros_like(acc)
    cov[...] = jnp.zeros_like(cov)
    row_ids = chunk * rows + lax.broadcasted_iota(jnp.int32, (rows, 128), 0)
    if first:
        for copy in copies:
            copy.wait()
    for source in range(sky):
        group, at = (0, source) if plan["single"] else (source, 0)
        for rank in range(cap):
            local = facts[0][source, 8 * rank]

            @pl.when(local >= 0)
            def _(group=group, at=at, rank=rank, source=source, local=local):
                start = plan["starts"][phase][group] + rank * rows
                acc[local] += boxes[group][at, start : start + rows, :].astype(F32)
                weight = jnp.full((rows, 128), facts[1][source, 8 * rank + 2], F32)
                cov[local] += jnp.where(row_ids < facts[0][source, 8 * rank + 1], weight, 0.0)

    width = acc.shape[2]
    for patch in range(per):
        factor = 1.0 / jnp.maximum(cov[patch], 1.0)
        for at in range(0, width, 128):
            value = acc[patch, :, at : at + 128] * factor
            acc[patch, :, at : at + 128] = value
            for other in arrived:
                value = value + other[patch, :, at : at + 128].astype(F32)
            extra[patch, :, at : at + 128] = value.astype(extra.dtype)
        if last:
            writes.append(pltpu.make_async_copy(acc.at[patch], out_rows(patch, phase), sems.at[phase, patch]))
            writes[-1].start()
    for write in writes:
        write.wait()


def band_plan(nb):
    shifts = list(range(1, nb)) + [0]
    return lambda band, phase: (
        (band + shifts[phase]) % nb if isinstance(band, int) else lax.rem(band + shifts[phase], nb)
    )


def copy_kernel(source, out):
    out[...] = source[...]


def brought(array):
    return pl.pallas_call(
        copy_kernel, out_shape=jax.ShapeDtypeStruct(array.shape, array.dtype),
        compiler_params=pltpu.CompilerParams(vmem_limit_bytes=SUM_VMEM * MIB), name="bring",
    )(array)


def accumulate_kernel(*refs):
    total, *terms, out, held, sems = refs
    copies = []
    for patch in range(total.shape[0]):
        value = total[patch]
        for term in terms:
            value = value + term[patch].astype(F32)
        held[patch] = value
        copies.append(pltpu.make_async_copy(held.at[patch], out.at[patch], sems.at[patch]))
        copies[-1].start()
    for copy in copies:
        copy.wait()


def per_device(patches, valid_rows, slot_owner, slot_local, slot_visit, basis_coef, inv_var, kernel_x, kernel_y):
    tiles = patches[0]
    slots, side, width = tiles.shape
    sky, nb = lax.axis_size("sky"), lax.axis_size("band")
    cap = max(2, 2 * slots // sky)
    rows = side // nb
    single = sky != 4
    tables = wave_tables(side, kernel_x.shape[1])
    sub, lane = tables["sub"], tables["lane"]
    chunk = band_plan(nb)
    late = min(3, nb - 1)
    adds = [[]] * (nb - 1) + [list(range(nb - 1 - late))]
    box = cap * rows
    shaped = lambda count, height: jax.ShapeDtypeStruct((count, height, width), BF16)
    if single:
        out_shapes = [shaped(sky, box + (HEAD if phase == 0 else 0)) for phase in range(nb)]
        place = lambda outs, dest, phase: (outs[phase], dest, 0)
        head = lambda outs, dest: (outs[0], dest, box)
    else:
        far = lambda phase: shaped(1, box + (HEAD if phase == 0 else 0))
        out_shapes = [shaped(1, nb * box + HEAD)] * 2 + [far(phase) for phase in range(nb) for _ in range(2)]

        def place(outs, dest, phase):
            return (outs[dest], 0, phase * box) if dest < 2 else (outs[2 * phase + dest], 0, 0)

        def head(outs, dest):
            return outs[dest], 0, nb * box if dest < 2 else box

    plan = dict(sub=sub, lane=lane, rows=rows, nb=nb, scale=tables["scale"], slots=slots, cap=cap, sky=sky, per=PATCH_DEV,
                single=single, n_boxes=1 if single else sky, place=place, head=head, chunk=chunk, adds=adds)
    smem = pl.BlockSpec(memory_space=pltpu.SMEM)
    hbm = pl.BlockSpec(memory_space=pltpu.HBM)
    consts = [jnp.asarray(tables[n]) for n in ("to_col", "to_row", "from_col", "from_row", "tap_col", "tap_row")]
    args = [slot_owner.reshape(1, slots), slot_local, valid_rows, slot_visit, inv_var, basis_coef.transpose(1, 0, 2),
            kernel_x, kernel_y] + consts + [tiles]
    plan.update(n_in=len(args), n_out=len(out_shapes))
    landing = [pltpu.SMEM(a.shape, a.dtype) for a in args[:5]] + [pltpu.VMEM(a.shape, a.dtype) for a in args[5:]]
    sent = pl.pallas_call(
        functools.partial(convolve_kernel, plan),
        out_shape=out_shapes,
        in_specs=[hbm] * len(args),
        out_specs=[hbm] * len(out_shapes),
        scratch_shapes=landing + [
            pltpu.SemaphoreType.DMA((max(len(args) - 1 + slots, sky),)), pltpu.SemaphoreType.DMA((slots, nb)),
            pltpu.VMEM((2 * sub, kernel_x.shape[0]), F32),
            pltpu.VMEM((kernel_x.shape[0], 2 * lane), BF16), pltpu.VMEM((side, 2 * sub), BF16),
            pltpu.VMEM((sky, 1, 128), F32),
            pltpu.VMEM((slots, side, width), BF16), pltpu.VMEM((sky, HEAD, width), BF16)],
        compiler_params=pltpu.CompilerParams(vmem_limit_bytes=CONV_VMEM * MIB),
        cost_estimate=pl.CostEstimate(flops=slots * 22 * side**3, bytes_accessed=slots * side * side * 6,
                                      transcendentals=0),
        name="convolve",
    )(*args)

    swap = lambda a, r: a if r == 0 else lax.ppermute(a, "sky", [(i, i ^ r) for i in range(sky)])
    if single:
        moved = [lax.all_to_all(s, "sky", split_axis=0, concat_axis=0, tiled=True) for s in sent]
        pieces = lambda phase: [(moved[phase], sky, 0, 0, box)]
    else:
        own, second = lax.optimization_barrier((brought(sent[0]), sent[4]))
        near = swap(sent[1], 1)
        far = [swap(a, 2 + i % 2) for i, a in enumerate([*sent[2:4], second, *sent[5:]])]

        def pieces(phase):
            here = [(a, 1, 0, phase, nb * box) for a in (own, near)]
            return here + [(a, 1, 0, 0, box) for a in far[2 * phase : 2 * phase + 2]]

    facts, arrived, finished = None, [], []
    band_shape = jax.ShapeDtypeStruct((PATCH_DEV, side, width), F32)
    chunk_shape = (PATCH_DEV, rows, width)
    vmem = pl.BlockSpec(memory_space=pltpu.VMEM)
    plan.update(starts=[[p[3] * box for p in pieces(phase)] for phase in range(nb)], ends=[p[4] for p in pieces(0)])
    fact_shapes = [jax.ShapeDtypeStruct((sky, 128), jnp.int32), jax.ShapeDtypeStruct((sky, 128), F32)]
    for phase in range(nb):
        first, last = phase == 0, phase == nb - 1
        inputs, specs = [], []
        inputs += [piece[0] for piece in pieces(phase)]
        specs += [vmem] * len(inputs)
        for earlier in adds[phase]:
            inputs.append(arrived[earlier])
            specs.append(vmem)
        outs = [band_shape if last else jax.ShapeDtypeStruct(chunk_shape, F32),
                jax.ShapeDtypeStruct(chunk_shape, F32 if last else BF16)]
        out_specs = [hbm if last else vmem, vmem]
        scratch = [pltpu.VMEM(chunk_shape, F32), pltpu.SemaphoreType.DMA((nb, PATCH_DEV))] if last else []
        scratch.append(pltpu.VMEM((PATCH_DEV, rows, 128), F32))
        if first:
            outs, out_specs = outs + fact_shapes, out_specs + [smem] * 2
            scratch += [pltpu.SemaphoreType.DMA((2,))] + [pltpu.VMEM(s.shape, s.dtype) for s in fact_shapes]
        else:
            inputs, specs = inputs + facts, specs + [smem] * 2
        if last:
            inputs, specs = inputs + finished, specs + [vmem] * len(finished)
        summed, extra, *rest = pl.pallas_call(
            functools.partial(sum_kernel, plan, phase),
            out_shape=outs,
            in_specs=specs,
            out_specs=out_specs,
            scratch_shapes=scratch,
            compiler_params=pltpu.CompilerParams(vmem_limit_bytes=SUM_VMEM * MIB),
            cost_estimate=pl.CostEstimate(flops=4 * PATCH_DEV * rows * width,
                                          bytes_accessed=12 * PATCH_DEV * rows * width, transcendentals=0),
            name="add_up",
        )(*inputs)
        finished.append(summed)
        facts = rest if first else facts
        if not last:
            arrived.append(lax.ppermute(extra, "band", [(b, chunk(b, phase)) for b in range(nb)]))
    if late:
        terms = arrived[nb - 1 - late :]
        for i in range(late - 1):
            extra, terms[i] = lax.optimization_barrier((extra, terms[i]))
        extra = pl.pallas_call(
            accumulate_kernel, out_shape=jax.ShapeDtypeStruct(chunk_shape, F32),
            in_specs=[vmem] * (1 + late), out_specs=hbm,
            scratch_shapes=[pltpu.VMEM(chunk_shape, F32), pltpu.SemaphoreType.DMA((PATCH_DEV,))],
            compiler_params=pltpu.CompilerParams(vmem_limit_bytes=SUM_VMEM * MIB), name="accumulate",
        )(extra, *terms)
    return (summed[None], extra)


def solution(mesh):
    in_specs = (
        P(("tract", "band"), "sky", None, None),
        P(("tract", "band"), "sky"),
        P(("tract", "band"), "sky", None),
        P(("tract", "band"), "sky"),
        P(("tract", "band"), "sky"),
        P(("tract", "band"), None, None),
        P(("tract", "band"), None),
        P(),
        P(),
    )
    out_specs = (P(("tract", "band"), "sky", None, None), P(("tract", "sky"), "band", None))
    return jax.shard_map(per_device, mesh=mesh, in_specs=in_specs, out_specs=out_specs, check_vma=False)
```

```python
import functools

import jax
import jax.numpy as jnp
import ml_dtypes
import numpy as np
from jax import lax
from jax.experimental import pallas as pl
from jax.experimental.pallas import tpu as pltpu
from jax.sharding import PartitionSpec as P

PATCH_DEV = 8
F32, BF16 = jnp.float32, jnp.bfloat16
MIB = 1024 * 1024
HEAD = 16
BATCH = 4
CONV_VMEM = 64
SUM_VMEM = 24


def round_up(value, multiple):
    return -(-value // multiple) * multiple


def wave_tables(side, kernel_len):
    half_len = kernel_len // 2
    count = -(-(side + half_len) // 2)
    omega = np.pi * (np.arange(count) + 0.5) / count
    sub, lane = round_up(count, 16), round_up(count, 128)

    def waves(points, width):
        out = np.zeros((len(points), 2 * width), np.float64)
        out[:, :count] = np.cos(np.outer(points, omega))
        out[:, width : width + count] = np.sin(np.outer(points, omega))
        return out

    pixels, taps = np.arange(side), np.arange(kernel_len) - half_len
    held = lambda a: np.ascontiguousarray(a).astype(ml_dtypes.bfloat16)
    return dict(
        sub=sub,
        lane=lane,
        scale=1.0 / (count * count),
        to_col=held(waves(pixels, lane)),
        to_row=held(waves(pixels, sub).T),
        from_col=held(waves(pixels, lane).T),
        from_row=held(waves(pixels, sub)),
        tap_col=held(waves(taps, lane)),
        tap_row=held(waves(taps, sub).T),
    )


def dot(a, b, contract=((1,), (0,))):
    return lax.dot_general(a, b, (contract, ((), ())), preferred_element_type=F32)


def weigh(waves, tables):
    sub, lane = tables.shape[0] // 2, tables.shape[1] // 2
    (cc, cs), (sc, ss) = [(a[:, :lane], a[:, lane:]) for a in waves]
    pa, pb, qa, qb = tables[:sub, :lane], tables[:sub, lane:], tables[sub:, :lane], tables[sub:, lane:]
    return (
        (pa * cc + pb * cs + qa * sc + qb * ss).astype(BF16),
        (pa * cs - pb * cc + qa * ss - qb * sc).astype(BF16),
        (pa * sc + pb * ss - qa * cc - qb * cs).astype(BF16),
        (pa * ss - pb * sc - qa * cs + qb * cc).astype(BF16),
    )


def convolve_kernel(plan, *refs):
    n_in, n_out = plan["n_in"], plan["n_out"]
    sources, outs, held = refs[:n_in], refs[n_in : n_in + n_out], refs[n_in + n_out :]
    local, (sems, out_sems, row_waves, col_waves, back, heads, done, head_rows) = held[:n_in], held[n_in:]
    sub, lane, rows, nb, cap, slots = (plan[k] for k in ("sub", "lane", "rows", "nb", "cap", "slots"))
    copies = [pltpu.make_async_copy(a, b, sems.at[i]) for i, (a, b) in enumerate(zip(sources[:-1], local[:-1]))]
    tiles = [
        pltpu.make_async_copy(sources[-1].at[s], local[-1].at[s], sems.at[n_in - 1 + s]) for s in range(slots)
    ]
    early, large = copies[:8] + copies[12:], copies[8:12]
    for copy in early + large + tiles:
        copy.start()
    owner, local_id, valid, visit, inv_var, coef, kx, ky, to_col, to_row, from_col, from_row, tap_col, tap_row, patch = local
    for copy in early:
        copy.wait()
    side = patch.shape[1]
    row_waves[...] = dot(tap_row[...], ky[...], ((1,), (1,)))
    col_waves[...] = (dot(kx[...], tap_col[...]) * plan["scale"]).astype(BF16)
    band = lax.axis_index("band")
    def place_back():
        for phase in range(nb):
            start = pl.multiple_of(plan["chunk"](band, phase) * rows, rows)
            back[phase * rows : (phase + 1) * rows, :] = from_row[pl.ds(start, rows), :]

    heads[...] = jnp.full(heads.shape, -1.0, F32)
    me = lax.axis_index("sky")
    basis = kx.shape[0]
    lanes = lax.broadcasted_iota(jnp.int32, (1, 128), 1)

    row_ids = lax.broadcasted_iota(jnp.int32, (side, side), 0)

    def mixing(slot):
        seen = visit[0, slot]
        weight = jnp.full((1, basis), inv_var[0, seen], F32).astype(BF16).astype(F32)
        return (weight * coef[seen].astype(BF16).astype(F32)).astype(BF16).astype(F32)

    def sent(slot, phase, ref):
        return pltpu.make_async_copy(done.at[slot, phase * rows : (phase + 1) * rows, :], ref, out_sems.at[slot, phase])

    def deliver(slot, full):
        done[slot] = full
        mine = owner[0, slot]
        rank = jnp.int32(0)
        for other in range(slots):
            rank = rank + jnp.where((other < slot) & (owner[0, other] == mine), 1, 0).astype(jnp.int32)
        box = mine if plan["single"] else mine ^ me
        weight = jnp.full((1, 128), inv_var[0, visit[0, slot]], F32)
        facts = jnp.where(lanes == 8 * rank, local_id[0, slot].astype(F32), heads[box])
        facts = jnp.where(lanes == 8 * rank + 1, valid[0, slot].astype(F32), facts)
        heads[box] = jnp.where(lanes == 8 * rank + 2, weight, facts)
        def store(box):
            for phase in range(nb):
                ref, at, first = plan["place"](outs, box, phase)
                start = pl.multiple_of(first + rank * rows, rows)
                sent(slot, phase, ref.at[at, pl.ds(start, rows), :]).start()

        if plan["single"]:
            store(mine)
        else:
            for index in range(plan["sky"]):
                pl.when(box == index)(functools.partial(store, index))

    mixed = [(row_waves[...] * mixing(s)).astype(BF16) for s in range(slots)]
    all_tables = dot(jnp.concatenate(mixed, axis=0), col_waves[...])
    for copy in large:
        copy.wait()
    place_back()
    for batch in range(0, slots, BATCH):
        group = range(batch, min(batch + BATCH, slots))
        for s in group:
            tiles[s].wait()
        masked = [jnp.where(row_ids < valid[0, s], patch[s], 0.0).astype(BF16) for s in group]
        col = dot(jnp.concatenate(masked, axis=0), to_col[...]).astype(BF16)
        tables = all_tables[batch * 2 * sub : (batch + len(group)) * 2 * sub]
        cos, sin = [], []
        for n, s in enumerate(group):
            mine = col[n * side : (n + 1) * side]
            both = dot(to_row[...], mine)
            y_cc, y_cs, y_sc, y_ss = weigh((both[:sub], both[sub:]), tables[n * 2 * sub : (n + 1) * 2 * sub])
            cos, sin = cos + [y_cc, y_sc], sin + [y_cs, y_ss]
        half = dot(jnp.concatenate(cos, axis=0), from_col[:lane, :])
        half = half + dot(jnp.concatenate(sin, axis=0), from_col[lane:, :])
        half = half.astype(BF16)
        for n, s in enumerate(group):
            full = dot(back[...], half[n * 2 * sub : (n + 1) * 2 * sub])
            deliver(s, full.astype(BF16))
    width = patch.shape[2]
    copies = []
    for index in range(plan["sky"]):
        ref, at, first = plan["head"](outs, index)
        row = jnp.concatenate([heads[index]] * (width // 128), axis=1)
        head_rows[index] = jnp.broadcast_to(row, (HEAD, width)).astype(BF16)
        copies.append(pltpu.make_async_copy(head_rows.at[index], ref.at[at, first : first + HEAD, :], sems.at[index]))
        copies[-1].start()
    for copy in copies:
        copy.wait()
    for slot in range(slots):
        for phase in range(nb):
            sent(slot, phase, plan["place"](outs, 0, phase)[0].at[0, 0:rows, :]).wait()


def sum_kernel(plan, phase, *refs):
    sky, nb, rows, cap, per = plan["sky"], plan["nb"], plan["rows"], plan["cap"], plan["per"]
    first, last = phase == 0, phase == nb - 1
    refs = list(refs)
    take = lambda n: [refs.pop(0) for _ in range(n)]
    boxes = take(plan["n_boxes"])
    arrived = take(len(plan["adds"][phase]))
    facts = None if first else take(2)
    earlier = take(nb - 1) if last else []
    if last:
        band_out, extra = take(2)
    else:
        acc, extra = take(2)
    if first:
        facts = take(2)
    if last:
        acc, sems = take(2)
    (cov,) = take(1)
    if first:
        (fact_sems,) = take(1)
    if first:
        whole_facts, weights = take(2)
        rows_of = []
        for source in range(sky):
            group, at = (0, source) if plan["single"] else (source, 0)
            rows_of.append(boxes[group][at, plan["ends"][group] : plan["ends"][group] + HEAD, :128][0:1].astype(F32))
        for source, row in enumerate(rows_of):
            whole_facts[source : source + 1, :] = row.astype(jnp.int32)
            weights[source : source + 1, :] = row
        copies = [pltpu.make_async_copy(a, b, fact_sems.at[i]) for i, (a, b) in enumerate(((whole_facts, facts[0]), (weights, facts[1])))]
        for copy in copies:
            copy.start()
    band = lax.axis_index("band")
    chunk = plan["chunk"](band, phase)

    def out_rows(patch, at):
        return band_out.at[patch, pl.ds(pl.multiple_of(plan["chunk"](band, at) * rows, rows), rows), :]

    writes = []
    for at, done in enumerate(earlier):
        for patch in range(per):
            writes.append(pltpu.make_async_copy(done.at[patch], out_rows(patch, at), sems.at[at, patch]))
            writes[-1].start()
    acc[...] = jnp.zeros_like(acc)
    cov[...] = jnp.zeros_like(cov)
    row_ids = chunk * rows + lax.broadcasted_iota(jnp.int32, (rows, 128), 0)
    if first:
        for copy in copies:
            copy.wait()
    for source in range(sky):
        group, at = (0, source) if plan["single"] else (source, 0)
        for rank in range(cap):
            local = facts[0][source, 8 * rank]

            @pl.when(local >= 0)
            def _(group=group, at=at, rank=rank, source=source, local=local):
                start = plan["starts"][phase][group] + rank * rows
                acc[local] += boxes[group][at, start : start + rows, :].astype(F32)
                weight = jnp.full((rows, 128), facts[1][source, 8 * rank + 2], F32)
                cov[local] += jnp.where(row_ids < facts[0][source, 8 * rank + 1], weight, 0.0)

    width = acc.shape[2]
    for patch in range(per):
        factor = 1.0 / jnp.maximum(cov[patch], 1.0)
        for at in range(0, width, 128):
            value = acc[patch, :, at : at + 128] * factor
            acc[patch, :, at : at + 128] = value
            for other in arrived:
                value = value + other[patch, :, at : at + 128].astype(F32)
            extra[patch, :, at : at + 128] = value.astype(extra.dtype)
        if last:
            writes.append(pltpu.make_async_copy(acc.at[patch], out_rows(patch, phase), sems.at[phase, patch]))
            writes[-1].start()
    for write in writes:
        write.wait()


def band_plan(nb):
    shifts = list(range(1, nb)) + [0]
    return lambda band, phase: (
        (band + shifts[phase]) % nb if isinstance(band, int) else lax.rem(band + shifts[phase], nb)
    )


def copy_kernel(source, out):
    out[...] = source[...]


def brought(array):
    return pl.pallas_call(
        copy_kernel, out_shape=jax.ShapeDtypeStruct(array.shape, array.dtype),
        compiler_params=pltpu.CompilerParams(vmem_limit_bytes=SUM_VMEM * MIB), name="bring",
    )(array)


def accumulate_kernel(*refs):
    total, *terms, out, held, sems = refs
    copies = []
    for patch in range(total.shape[0]):
        value = total[patch]
        for term in terms:
            value = value + term[patch].astype(F32)
        held[patch] = value
        copies.append(pltpu.make_async_copy(held.at[patch], out.at[patch], sems.at[patch]))
        copies[-1].start()
    for copy in copies:
        copy.wait()


def per_device(patches, valid_rows, slot_owner, slot_local, slot_visit, basis_coef, inv_var, kernel_x, kernel_y):
    tiles = patches[0]
    slots, side, width = tiles.shape
    sky, nb = lax.axis_size("sky"), lax.axis_size("band")
    cap = max(2, 2 * slots // sky)
    rows = side // nb
    single = sky != 4
    tables = wave_tables(side, kernel_x.shape[1])
    sub, lane = tables["sub"], tables["lane"]
    chunk = band_plan(nb)
    late = min(3, nb - 1)
    adds = [[]] * (nb - 1) + [list(range(nb - 1 - late))]
    box = cap * rows
    shaped = lambda count, height: jax.ShapeDtypeStruct((count, height, width), BF16)
    if single:
        out_shapes = [shaped(sky, box + (HEAD if phase == 0 else 0)) for phase in range(nb)]
        place = lambda outs, dest, phase: (outs[phase], dest, 0)
        head = lambda outs, dest: (outs[0], dest, box)
    else:
        far = lambda phase: shaped(1, box + (HEAD if phase == 0 else 0))
        out_shapes = [shaped(1, nb * box + HEAD)] * 2 + [far(phase) for phase in range(nb) for _ in range(2)]

        def place(outs, dest, phase):
            return (outs[dest], 0, phase * box) if dest < 2 else (outs[2 * phase + dest], 0, 0)

        def head(outs, dest):
            return outs[dest], 0, nb * box if dest < 2 else box

    plan = dict(sub=sub, lane=lane, rows=rows, nb=nb, scale=tables["scale"], slots=slots, cap=cap, sky=sky, per=PATCH_DEV,
                single=single, n_boxes=1 if single else sky, place=place, head=head, chunk=chunk, adds=adds)
    smem = pl.BlockSpec(memory_space=pltpu.SMEM)
    hbm = pl.BlockSpec(memory_space=pltpu.HBM)
    consts = [jnp.asarray(tables[n]) for n in ("to_col", "to_row", "from_col", "from_row", "tap_col", "tap_row")]
    args = [slot_owner.reshape(1, slots), slot_local, valid_rows, slot_visit, inv_var, basis_coef.transpose(1, 0, 2),
            kernel_x, kernel_y] + consts + [tiles]
    plan.update(n_in=len(args), n_out=len(out_shapes))
    landing = [pltpu.SMEM(a.shape, a.dtype) for a in args[:5]] + [pltpu.VMEM(a.shape, a.dtype) for a in args[5:]]
    sent = pl.pallas_call(
        functools.partial(convolve_kernel, plan),
        out_shape=out_shapes,
        in_specs=[hbm] * len(args),
        out_specs=[hbm] * len(out_shapes),
        scratch_shapes=landing + [
            pltpu.SemaphoreType.DMA((max(len(args) - 1 + slots, sky),)), pltpu.SemaphoreType.DMA((slots, nb)),
            pltpu.VMEM((2 * sub, kernel_x.shape[0]), F32),
            pltpu.VMEM((kernel_x.shape[0], 2 * lane), BF16), pltpu.VMEM((side, 2 * sub), BF16),
            pltpu.VMEM((sky, 1, 128), F32),
            pltpu.VMEM((slots, side, width), BF16), pltpu.VMEM((sky, HEAD, width), BF16)],
        compiler_params=pltpu.CompilerParams(vmem_limit_bytes=CONV_VMEM * MIB),
        cost_estimate=pl.CostEstimate(flops=slots * 22 * side**3, bytes_accessed=slots * side * side * 6,
                                      transcendentals=0),
        name="convolve",
    )(*args)

    swap = lambda a, r: a if r == 0 else lax.ppermute(a, "sky", [(i, i ^ r) for i in range(sky)])
    if single:
        moved = [lax.all_to_all(s, "sky", split_axis=0, concat_axis=0, tiled=True) for s in sent]
        pieces = lambda phase: [(moved[phase], sky, 0, 0, box)]
    else:
        own, second = lax.optimization_barrier((brought(sent[0]), sent[4]))
        near = swap(sent[1], 1)
        far = [swap(a, 2 + i % 2) for i, a in enumerate([*sent[2:4], second, *sent[5:]])]

        def pieces(phase):
            here = [(a, 1, 0, phase, nb * box) for a in (own, near)]
            return here + [(a, 1, 0, 0, box) for a in far[2 * phase : 2 * phase + 2]]

    facts, arrived, finished = None, [], []
    band_shape = jax.ShapeDtypeStruct((PATCH_DEV, side, width), F32)
    chunk_shape = (PATCH_DEV, rows, width)
    vmem = pl.BlockSpec(memory_space=pltpu.VMEM)
    plan.update(starts=[[p[3] * box for p in pieces(phase)] for phase in range(nb)], ends=[p[4] for p in pieces(0)])
    fact_shapes = [jax.ShapeDtypeStruct((sky, 128), jnp.int32), jax.ShapeDtypeStruct((sky, 128), F32)]
    for phase in range(nb):
        first, last = phase == 0, phase == nb - 1
        inputs, specs = [], []
        inputs += [piece[0] for piece in pieces(phase)]
        specs += [vmem] * len(inputs)
        for earlier in adds[phase]:
            inputs.append(arrived[earlier])
            specs.append(vmem)
        outs = [band_shape if last else jax.ShapeDtypeStruct(chunk_shape, F32),
                jax.ShapeDtypeStruct(chunk_shape, F32 if last else BF16)]
        out_specs = [hbm if last else vmem, vmem]
        scratch = [pltpu.VMEM(chunk_shape, F32), pltpu.SemaphoreType.DMA((nb, PATCH_DEV))] if last else []
        scratch.append(pltpu.VMEM((PATCH_DEV, rows, 128), F32))
        if first:
            outs, out_specs = outs + fact_shapes, out_specs + [smem] * 2
            scratch += [pltpu.SemaphoreType.DMA((2,))] + [pltpu.VMEM(s.shape, s.dtype) for s in fact_shapes]
        else:
            inputs, specs = inputs + facts, specs + [smem] * 2
        if last:
            inputs, specs = inputs + finished, specs + [vmem] * len(finished)
        summed, extra, *rest = pl.pallas_call(
            functools.partial(sum_kernel, plan, phase),
            out_shape=outs,
            in_specs=specs,
            out_specs=out_specs,
            scratch_shapes=scratch,
            compiler_params=pltpu.CompilerParams(vmem_limit_bytes=SUM_VMEM * MIB),
            cost_estimate=pl.CostEstimate(flops=4 * PATCH_DEV * rows * width,
                                          bytes_accessed=12 * PATCH_DEV * rows * width, transcendentals=0),
            name="add_up",
        )(*inputs)
        finished.append(summed)
        facts = rest if first else facts
        if not last:
            arrived.append(lax.ppermute(extra, "band", [(b, chunk(b, phase)) for b in range(nb)]))
    if late:
        terms = arrived[nb - 1 - late :]
        for i in range(late - 1):
            extra, terms[i] = lax.optimization_barrier((extra, terms[i]))
        extra = pl.pallas_call(
            accumulate_kernel, out_shape=jax.ShapeDtypeStruct(chunk_shape, F32),
            in_specs=[vmem] * (1 + late), out_specs=hbm,
            scratch_shapes=[pltpu.VMEM(chunk_shape, F32), pltpu.SemaphoreType.DMA((PATCH_DEV,))],
            compiler_params=pltpu.CompilerParams(vmem_limit_bytes=SUM_VMEM * MIB), name="accumulate",
        )(extra, *terms)
    return (summed[None], extra)


def solution(mesh):
    in_specs = (
        P(("tract", "band"), "sky", None, None),
        P(("tract", "band"), "sky"),
        P(("tract", "band"), "sky", None),
        P(("tract", "band"), "sky"),
        P(("tract", "band"), "sky"),
        P(("tract", "band"), None, None),
        P(("tract", "band"), None),
        P(),
        P(),
    )
    out_specs = (P(("tract", "band"), "sky", None, None), P(("tract", "sky"), "band", None))
    return jax.shard_map(per_device, mesh=mesh, in_specs=in_specs, out_specs=out_specs, check_vma=False)
```
